128 devices in a mesh: sec: 2 (over z_hi), ctx: 16 (over y, z_lo, core), tp: 4 (over x).
Axes of the slice: x: 4, y: 4, z: 4 (z_hi: 2, z_lo: 2; z = z_hi * 2 + z_lo), core: 2. Of those that a mesh axis runs over, the one named last changes fastest.
Arguments:
- p_query: bfloat16 [2, 8, 512, 3584], P('sec', None, 'ctx', 'tp'), may hold values from -3 to 3
- p_key: bfloat16 [2, 8, 512, 512], P('sec', None, 'ctx', 'tp'), may hold values from -1.5 to 1.5
- p_value: bfloat16 [2, 8, 512, 512], P('sec', None, 'ctx', 'tp'), may hold values from -6 to 6
- p_cache_k: bfloat16 [2, 384, 128, 512], P('sec', 'ctx', None, 'tp'), may hold values from -1.5 to 1.5
- p_cache_v: bfloat16 [2, 384, 128, 512], P('sec', 'ctx', None, 'tp'), may hold values from -6 to 6
- p_slot_req: int32 [2, 384], P('sec', 'ctx'), may hold values from 0 to 7, as said below
- p_slot_blk: int32 [2, 384], P('sec', 'ctx'), may hold values from 0 to 191, as said below
- p_offsets: int32 [2, 8], P('sec'), may hold values from 1 to 24576, as said below
- d_query: bfloat16 [2, 32, 4, 3584], P('sec', 'ctx', None, 'tp'), may hold values from -3 to 3
- d_key: bfloat16 [2, 32, 4, 512], P('sec', 'ctx', None, 'tp'), may hold values from -1.5 to 1.5
- d_value: bfloat16 [2, 32, 4, 512], P('sec', 'ctx', None, 'tp'), may hold values from -6 to 6
- d_cache_k: bfloat16 [2, 384, 128, 512], P('sec', 'ctx', None, 'tp'), may hold values from -1.5 to 1.5
- d_cache_v: bfloat16 [2, 384, 128, 512], P('sec', 'ctx', None, 'tp'), may hold values from -6 to 6
- d_slot_req: int32 [2, 384], P('sec', 'ctx'), may hold values from 0 to 31, as said below
- d_slot_blk: int32 [2, 384], P('sec', 'ctx'), may hold values from 0 to 191, as said below
- d_lengths: int32 [2, 32], P('sec'), may hold values from 1 to 24576, as said below
- out_weight: bfloat16 [3584, 7168], P('tp'), may hold values from -1 to 1
Outputs:
- prefill_out: bfloat16 [2, 8, 512, 7168], P('sec', None, 'ctx', 'tp')
- decode_out: bfloat16 [2, 32, 4, 7168], P('sec', 'ctx', None, 'tp')
The draws below stay inside these ranges and needn't reach their ends.
Inputs may be any that keep to these rules, and one draw needn't show every extreme that they name: `p_slot_req`: in each section every one of the 384 slots holds a block of one of the 8 requests, and every request holds at least one block. `p_slot_blk`: in each section the blocks of a request are numbered from 0 to its block count minus 1, each held by exactly one slot; one request holds exactly 192 blocks, and no request holds more. `p_offsets`: A request with c blocks has an offset from (c - 1) * 128 + 1 to c * 128. `d_slot_req`: in each section every one of the 384 slots holds a block of one of the 32 requests, and every request holds at least one block. `d_slot_blk`: in each section the blocks of a request are numbered from 0 to its block count minus 1, each held by exactly one slot; one request holds exactly 192 blocks, and no request holds more. `d_lengths`: A request with c blocks has a length from (c - 1) * 128 + 1 to c * 128.
All inputs are finite; a program needn't handle non-finite values.
Results may differ from the reference program's by a relative error of at most 0.025.
Values may be sent and summed in bfloat16 or wider, within the bound.
No kernel may reach another device: no remote copies, remote signals or barrier semaphores. Data moves between devices by JAX's collectives and lax.ppermute only.
A program may use at most 192 MiB of HBM per device.

```python
from functools import partial
import jax
import jax.numpy as jnp
from jax import lax

D = 7168
HEADS = 28
KVH = 4
HD = 128
PAGE = 128
P_REQ = 8
STEPS = 4
SECS = 2
SPAN = 512
D_REQ = 32
PBLOCKS = 384
DBLOCKS = 384


def section_tables(key, req_count, block_count):
    first, second, third, fourth = jax.random.split(key, 4)
    biggest = block_count - block_count // 2
    rest = block_count // 2
    cuts = jnp.sort(jax.random.permutation(first, rest - 1)[:req_count - 2] + 1).astype(jnp.int32)
    small_bounds = jnp.concatenate([jnp.zeros((1,), jnp.int32), cuts, jnp.full((1,), rest, jnp.int32)])
    small_counts = small_bounds[1:] - small_bounds[:-1]
    chosen = jax.random.randint(fourth, (), 0, req_count, dtype=jnp.int32)
    requests = jnp.arange(req_count, dtype=jnp.int32)
    lower_idx = jnp.clip(requests, 0, req_count - 2)
    upper_idx = jnp.clip(requests - 1, 0, req_count - 2)
    counts = jnp.where(requests < chosen, small_counts[lower_idx], jnp.where(requests == chosen, biggest, small_counts[upper_idx])).astype(jnp.int32)
    ends = jnp.cumsum(counts).astype(jnp.int32)
    starts = ends - counts
    blocks = jnp.arange(block_count, dtype=jnp.int32)
    owners = jnp.sum((blocks[:, None] >= ends[None, :]).astype(jnp.int32), axis=1)
    matches = (owners[:, None] == requests[None, :]).astype(jnp.int32)
    ranks = blocks - jnp.sum(matches * starts[None, :], axis=1)
    placed = jax.random.permutation(second, block_count).astype(jnp.int32)
    trims = jax.random.randint(third, (req_count,), 0, PAGE, dtype=jnp.int32)
    trims = jnp.where(requests == chosen, 0, trims)
    return (owners[placed], ranks[placed], counts * PAGE - trims)


def all_tables(key, salt, req_count, block_count):
    section_keys = jax.random.split(jax.random.fold_in(key, salt), SECS)
    return jax.vmap(partial(section_tables, req_count=req_count, block_count=block_count))(section_keys)


def draw_p_slot_req(key, part):
    tables = all_tables(key, 101, P_REQ, PBLOCKS)
    return tables[0]


def draw_p_slot_blk(key, part):
    tables = all_tables(key, 101, P_REQ, PBLOCKS)
    return tables[1]


def draw_p_offsets(key, part):
    tables = all_tables(key, 101, P_REQ, PBLOCKS)
    return tables[2]


def draw_d_slot_req(key, part):
    tables = all_tables(key, 202, D_REQ, DBLOCKS)
    return tables[0]


def draw_d_slot_blk(key, part):
    tables = all_tables(key, 202, D_REQ, DBLOCKS)
    return tables[1]


def draw_d_lengths(key, part):
    tables = all_tables(key, 202, D_REQ, DBLOCKS)
    return tables[2]


def levels(own_key, dims, cuts, least, top_value):
    loudness, own = 1.0, jax.random.fold_in(own_key, 6)
    for position, parts in cuts:
        draws = jnp.exp(jax.random.uniform(jax.random.fold_in(own, position), (parts,), jnp.float32, least / len(cuts), top_value / len(cuts)))
        loudness = loudness * jnp.repeat(draws, dims[position] // parts).reshape([-1 if axis == position else 1 for axis in range(len(dims))])
    return loudness


def noise(rng, dims, scale, most, cuts=(), kind=jnp.bfloat16):
    entries = scale * jax.random.normal(rng, dims, jnp.float32)
    if cuts:
        entries = entries * levels(rng, dims, cuts, -0.22, 0.18)
    return jnp.clip(entries, -most, most).astype(kind)


def setup_inputs(seed: int = 0) -> dict:
    seeds = jax.random.split(jax.random.key(seed), 18)
    p_query = jnp.clip(jax.random.uniform(seeds[0], (SECS, P_REQ, SPAN, HEADS * HD), jnp.float32, -3.0, 3.0) * levels(seeds[0], (SECS, P_REQ, SPAN, HEADS * HD), ((0, 2), (2, 16), (3, 4)), -0.4, 0.0), -3.0, 3.0).astype(jnp.bfloat16)
    p_key = jnp.clip(jax.random.uniform(seeds[1], (SECS, P_REQ, SPAN, KVH * HD), jnp.float32, -1.5, 1.5) * levels(seeds[1], (SECS, P_REQ, SPAN, KVH * HD), ((0, 2), (2, 16), (3, 4)), -0.4, 0.0), -1.5, 1.5).astype(jnp.bfloat16)
    p_value = noise(seeds[2], (SECS, P_REQ, SPAN, KVH * HD), 1.0, 6.0, ((0, 2), (2, 16), (3, 4)))
    p_cache_k = jnp.clip(jax.random.uniform(seeds[3], (SECS, PBLOCKS, PAGE, KVH * HD), jnp.float32, -1.5, 1.5) * levels(seeds[3], (SECS, PBLOCKS, PAGE, KVH * HD), ((0, 2), (1, 16), (3, 4)), -0.4, 0.0), -1.5, 1.5).astype(jnp.bfloat16)
    p_cache_v = noise(seeds[4], (SECS, PBLOCKS, PAGE, KVH * HD), 1.0, 6.0, ((0, 2), (1, 16), (3, 4)))
    p_slot_req = draw_p_slot_req(jax.random.fold_in(seeds[17], 71), 0)
    p_slot_blk = draw_p_slot_blk(jax.random.fold_in(seeds[17], 71), 0)
    p_offsets = draw_p_offsets(jax.random.fold_in(seeds[17], 71), 0)
    d_query = jnp.clip(jax.random.uniform(seeds[8], (SECS, D_REQ, STEPS, HEADS * HD), jnp.float32, -3.0, 3.0) * levels(seeds[8], (SECS, D_REQ, STEPS, HEADS * HD), ((0, 2), (1, 16), (3, 4)), -0.4, 0.0), -3.0, 3.0).astype(jnp.bfloat16)
    d_key = jnp.clip(jax.random.uniform(seeds[9], (SECS, D_REQ, STEPS, KVH * HD), jnp.float32, -1.5, 1.5) * levels(seeds[9], (SECS, D_REQ, STEPS, KVH * HD), ((0, 2), (1, 16), (3, 4)), -0.4, 0.0), -1.5, 1.5).astype(jnp.bfloat16)
    d_value = noise(seeds[10], (SECS, D_REQ, STEPS, KVH * HD), 1.0, 6.0, ((0, 2), (1, 16), (3, 4)))
    d_cache_k = jnp.clip(jax.random.uniform(seeds[11], (SECS, DBLOCKS, PAGE, KVH * HD), jnp.float32, -1.5, 1.5) * levels(seeds[11], (SECS, DBLOCKS, PAGE, KVH * HD), ((0, 2), (1, 16), (3, 4)), -0.4, 0.0), -1.5, 1.5).astype(jnp.bfloat16)
    d_cache_v = noise(seeds[12], (SECS, DBLOCKS, PAGE, KVH * HD), 1.0, 6.0, ((0, 2), (1, 16), (3, 4)))
    d_slot_req = draw_d_slot_req(jax.random.fold_in(seeds[17], 71), 0)
    d_slot_blk = draw_d_slot_blk(jax.random.fold_in(seeds[17], 71), 0)
    d_lengths = draw_d_lengths(jax.random.fold_in(seeds[17], 71), 0)
    out_weight = noise(seeds[16], (HEADS * HD, D), HEADS ** -0.5, 1.0, ((0, 4),))
    return dict(p_query=p_query, p_key=p_key, p_value=p_value, p_cache_k=p_cache_k, p_cache_v=p_cache_v, p_slot_req=p_slot_req, p_slot_blk=p_slot_blk, p_offsets=p_offsets, d_query=d_query, d_key=d_key, d_value=d_value, d_cache_k=d_cache_k, d_cache_v=d_cache_v, d_slot_req=d_slot_req, d_slot_blk=d_slot_blk, d_lengths=d_lengths, out_weight=out_weight)


def block_terms(queries, cache_keys, cache_values, slot_req, slot_blk, bounds):
    group_len = HEADS // KVH
    softmax_scale = HD ** -0.5
    req_count, new_count = queries.shape[0], queries.shape[1]
    shaped = queries.reshape(req_count, new_count, KVH, group_len, HD).astype(jnp.float32)
    within = jnp.arange(PAGE, dtype=jnp.int32)

    def advance(state, pieces):
        numerator, denominator = state
        key_blk, value_blk, owner_id, block_id = pieces
        chosen = lax.dynamic_index_in_dim(shaped, owner_id, 0, keepdims=False)
        key_rows = key_blk.reshape(PAGE, KVH, HD).astype(jnp.float32)
        value_rows = value_blk.reshape(PAGE, KVH, HD).astype(jnp.float32)
        scores = jnp.einsum("qhgd,khd->qhgk", chosen, key_rows) * softmax_scale
        limit_tok = lax.dynamic_index_in_dim(bounds, owner_id, 0, keepdims=False)
        visible = block_id * PAGE + within < limit_tok
        weights = jnp.where(visible, jnp.exp(scores), 0.0)
        rounded = lax.optimization_barrier(weights.astype(jnp.bfloat16)).astype(jnp.float32)
        products = jnp.einsum("qhgk,khd->qhgd", rounded, value_rows)
        numerator = numerator.at[owner_id].add(products)
        denominator = denominator.at[owner_id].add(jnp.sum(weights, axis=3))
        return (numerator, denominator), None

    start_num = jnp.zeros((req_count, new_count, KVH, group_len, HD), jnp.float32)
    start_den = jnp.zeros((req_count, new_count, KVH, group_len), jnp.float32)
    result, unused = lax.scan(advance, (start_num, start_den), (cache_keys, cache_values, slot_req, slot_blk))
    return result


def dense_terms(queries, keys, values, visible):
    group_len = HEADS // KVH
    req_count, new_count = queries.shape[0], queries.shape[1]
    shaped = queries.reshape(req_count, new_count, KVH, group_len, HD).astype(jnp.float32)
    key_rows = keys.reshape(req_count, keys.shape[1], KVH, HD).astype(jnp.float32)
    value_rows = values.reshape(req_count, values.shape[1], KVH, HD).astype(jnp.float32)
    scores = jnp.einsum("rqhgd,rkhd->rqhgk", shaped, key_rows) * HD ** -0.5
    weights = jnp.where(visible[None, :, None, None, :], jnp.exp(scores), 0.0)
    rounded = lax.optimization_barrier(weights.astype(jnp.bfloat16)).astype(jnp.float32)
    products = jnp.einsum("rqhgk,rkhd->rqhgd", rounded, value_rows)
    return products, jnp.sum(weights, axis=4)


def project(numerator, denominator, out_weight):
    attention = (numerator / denominator[..., None]).astype(jnp.bfloat16)
    flat_rows = attention.reshape(-1, HEADS * HD)
    return jnp.dot(flat_rows, out_weight, preferred_element_type=jnp.float32).astype(jnp.bfloat16)


def reference(p_query, p_key, p_value, p_cache_k, p_cache_v, p_slot_req, p_slot_blk, p_offsets, d_query, d_key, d_value, d_cache_k, d_cache_v, d_slot_req, d_slot_blk, d_lengths, out_weight):
    prefill_list = []
    decode_list = []
    causal_span = jnp.arange(SPAN)[:, None] >= jnp.arange(SPAN)[None, :]
    causal_steps = jnp.arange(STEPS)[:, None] >= jnp.arange(STEPS)[None, :]
    every_span = jnp.ones((STEPS, SPAN), dtype=bool)
    for section in range(SECS):
        partner = SECS - 1 - section
        numerator, denominator = block_terms(p_query[section], p_cache_k[section], p_cache_v[section], p_slot_req[section], p_slot_blk[section], p_offsets[section])
        products, weight_sums = dense_terms(p_query[section], p_key[section], p_value[section], causal_span)
        numerator = numerator + products
        denominator = denominator + weight_sums
        prefill_list.append(project(numerator, denominator, out_weight).reshape(P_REQ, SPAN, D))
        numerator, denominator = block_terms(d_query[section], d_cache_k[section], d_cache_v[section], d_slot_req[section], d_slot_blk[section], d_lengths[section])
        products, weight_sums = dense_terms(d_query[section][:P_REQ], p_key[partner], p_value[partner], every_span)
        numerator = numerator.at[:P_REQ].add(products)
        denominator = denominator.at[:P_REQ].add(weight_sums)
        products, weight_sums = dense_terms(d_query[section], d_key[section], d_value[section], causal_steps)
        numerator = numerator + products
        denominator = denominator + weight_sums
        decode_list.append(project(numerator, denominator, out_weight).reshape(D_REQ, STEPS, D))
    return jnp.stack(prefill_list), jnp.stack(decode_list)
```

```python
import functools

import jax
import jax.numpy as jnp
from jax import lax
from jax.experimental import pallas as pl
from jax.experimental.pallas import tpu as pltpu
from jax.sharding import PartitionSpec as P

HD = 128
PAGE = 128
BF = jnp.bfloat16
F32 = jnp.float32
NT = (((1,), (1,)), ((), ()))
NB = 4
VM = pl.BlockSpec(memory_space=pltpu.VMEM)
SM = pl.BlockSpec(memory_space=pltpu.SMEM)
HBM = pl.BlockSpec(memory_space=pl.ANY)


def attn_kernel(order, lim, starts, *refs, first, R, heads, half):
    rows=heads*128
    if first:
        bases, q0,q1,q2,q3, ka, kb, va, vb, sk, sv, num, den, ks, vs, qs, dacc, tile, sem = refs
    else:
        q0,q1,q2,q3, ka, kb, va, vb, num_in, den_in, o0,o1,o2,o3, ks, vs, qs, acc, dacc, sem = refs
    cs=[pltpu.make_async_copy(ka, ks.at[pl.ds(0,half)], sem.at[0]),
        pltpu.make_async_copy(kb, ks.at[pl.ds(half,half)], sem.at[1]),
        pltpu.make_async_copy(va, vs.at[pl.ds(0,half)], sem.at[2]),
        pltpu.make_async_copy(vb, vs.at[pl.ds(half,half)], sem.at[3])]
    for c in cs: c.start()
    qr=(q0,q1,q2,q3)
    for r in range(R):
        for h in range(heads):
            for d in range(4):
                qs[r,pl.ds(h*128+d*32,32),:]=qr[d][r,:,pl.ds(h*128,128)]
    if first:
        rowi=lax.broadcasted_iota(jnp.int32,(128,128),0); coli=lax.broadcasted_iota(jnp.int32,(128,128),1)
        def pick(i,b):
            g=i//32
            return jnp.where(g==0,bases[b],jnp.where(g==1,bases[b+1],jnp.where(g==2,bases[b+2],bases[b+3])))+lax.rem(i,32)
        tile[...]=jnp.where(pick(rowi,0)>=pick(coli,4),1.0,0.0)
    for c in cs: c.wait()
    lane1=lax.broadcasted_iota(jnp.int32,(128,128),1)
    lane=lax.broadcasted_iota(jnp.int32,(1,128),1)
    if first: den[...]=jnp.zeros_like(den)
    def request(r,dtile):
        s0=starts[r]; n=starts[r+1]-s0
        nref=num.at[r] if first else acc
        def fetch(i):
            ok=i<n
            s=jnp.where(ok,s0+i,0)
            b=order[s]
            return ks[b],vs[b],jnp.where(ok,lim[s],0)
        def weights(Ks,ms):
            K=jnp.concatenate(Ks,axis=0)
            sc=lax.dot_general(qs[r],K,NT,preferred_element_type=F32)
            w=jnp.exp(sc*HD**-0.5)
            return [m(w[:,j*128:(j+1)*128]) for j,m in enumerate(ms)]
        def keep(l):
            return lambda w: jnp.where(lane<l,w,0.0)
        def causal(w):
            return (w.reshape(heads,128,128)*tile[...][None]).reshape(rows,128)
        def causal_sel(w):
            return jnp.where(tile[...][None]>0.5,w.reshape(heads,128,128),0.0).reshape(rows,128)
        def total(ws):
            t=ws[0]
            for w in ws[1:]: t=t+w
            return t
        def product(ws,Vs):
            return jnp.dot(jnp.concatenate([w.astype(BF) for w in ws],axis=1),jnp.concatenate(Vs,axis=0),preferred_element_type=F32)
        skip=0
        if first:
            f=[fetch(i) for i in range(NB-1)]
            ws=weights([sk[r]]+[x[0] for x in f],[causal_sel]+[keep(x[2]) for x in f])
            dacc[...]=total(ws)
            nref[...]=product(ws,[sv[r]]+[x[1] for x in f])
            skip=NB-1
        else:
            acc[...]=jnp.zeros_like(acc); dacc[...]=jnp.zeros_like(dacc)
        def step(p,_):
            f=[fetch(skip+NB*p+i) for i in range(NB)]
            ws=weights([x[0] for x in f],[keep(x[2]) for x in f])
            dacc[...]+=total(ws)
            nref[...]+=product(ws,[x[1] for x in f])
            return 0
        lax.fori_loop(0,(jnp.maximum(n-skip,0)+NB-1)//NB,step,0)
        upd=dtile
        for h in range(heads):
            col=jnp.sum(dacc[pl.ds(h*128,128),:],axis=1,keepdims=True)
            upd=upd+jnp.where(lane1==r*16+h,col,0.0)
        if not first:
            outs=(o0,o1,o2,o3)
            for h in range(heads):
                for d in range(4):
                    sl=pl.ds(h*128+d*32,32)
                    outs[d][pl.ds(pl.multiple_of(r*32,32),32),pl.ds(h*128,128)]=(num_in[r,sl,:]+acc[sl,:]).astype(BF)
        return upd
    init=jnp.zeros((128,128),F32) if first else den_in[...]
    dl=lax.fori_loop(0,R,request,init)
    if first:
        den[...]=dl
    else:
        outs=(o0,o1,o2,o3)
        hi=dl.astype(BF)
        lo=(dl-hi.astype(F32)).astype(BF)
        for d in range(4):
            z=jnp.zeros((16,128),BF)
            for k,a in enumerate((hi,lo)):
                outs[d][R*32:R*32+16,pl.ds(k*256,128)]=a[d*32:d*32+16]
                outs[d][R*32:R*32+16,pl.ds(k*256+128,128)]=a[d*32+16:d*32+32]
            for k in range(4,heads):
                outs[d][R*32:R*32+16,pl.ds(k*128,128)]=z

def attn(first, order, lim, starts, qs, kv, extra):
    R,T,W=qs[0].shape
    heads=W//HD
    rows=heads*128
    nb=order.shape[0]
    half=nb//2
    anyspec=pl.BlockSpec(memory_space=pl.ANY)
    vm=pl.BlockSpec(memory_space=pltpu.VMEM)
    sm=pl.BlockSpec(memory_space=pltpu.SMEM)
    scr=[pltpu.VMEM((nb,128,128),BF),pltpu.VMEM((nb,128,128),BF),pltpu.VMEM((R,rows,128),BF)]
    cost=pl.CostEstimate(flops=4*nb*rows*128*128,bytes_accessed=12_000_000,transcendentals=nb*rows*128)
    body=functools.partial(attn_kernel,first=first,R=R,heads=heads,half=half)
    cp=pltpu.CompilerParams(vmem_limit_bytes=48<<20)
    if first:
        bases,sk,sv=extra
        return pl.pallas_call(body,in_specs=[sm]*4+[vm]*4+[anyspec]*4+[vm]*2,out_specs=[vm]*2,
            scratch_shapes=scr+[pltpu.VMEM((rows,128),F32),pltpu.VMEM((128,128),F32),pltpu.SemaphoreType.DMA((4,))],
            out_shape=[jax.ShapeDtypeStruct((R,rows,128),F32),jax.ShapeDtypeStruct((128,128),F32)],
            compiler_params=cp,cost_estimate=cost,name="attn_near")(order,lim,starts,bases,*qs,*kv,sk,sv)
    num,den=extra
    return pl.pallas_call(body,in_specs=[sm]*3+[vm]*4+[anyspec]*4+[vm]*2,out_specs=[vm]*4,
        scratch_shapes=scr+[pltpu.VMEM((rows,128),F32),pltpu.VMEM((rows,128),F32),pltpu.SemaphoreType.DMA((4,))],
        out_shape=[jax.ShapeDtypeStruct((R*T+16,W),BF)]*4,compiler_params=cp,cost_estimate=cost,name="attn_far")(order,lim,starts,*qs,*kv,num,den)


def decode_kernel(req, lim, ctx, q, k, v, hk, hv, dk, dv, out, acc, dacc):
    scale = HD ** -0.5
    blocks = k.shape[0]
    handed = hk.shape[0]
    lane = lax.broadcasted_iota(jnp.int32, (1, 128), 1)
    acc[...] = jnp.zeros_like(acc)
    dacc[...] = jnp.zeros_like(dacc)

    def block(i, unused):
        r = req[i]
        s = lax.dot_general(q[r], k[i], NT, preferred_element_type=F32)
        w = jnp.where(lane < lim[i], jnp.exp(s * scale), 0.0)
        dacc[r] += w
        acc[r] += jnp.dot(w.astype(BF), v[i], preferred_element_type=F32)
        return 0

    lax.fori_loop(0, blocks, block, 0, unroll=True)

    def first_lane(w):
        return jnp.where(lane == 0, jnp.sum(w, axis=1, keepdims=True), 0.0)

    for r in range(handed):
        s = lax.dot_general(q[r], hk[r], NT, preferred_element_type=F32)
        w = jnp.exp(s * scale)
        dacc[r] += first_lane(w)
        acc[r] += jnp.dot(w.astype(BF), hv[r], preferred_element_type=F32)
    steps = 4
    for j in range(dk.shape[0]):
        r = ctx[0] * dk.shape[0] + j
        s = lax.dot_general(q[r], dk[j], NT, preferred_element_type=F32)
        row = lax.rem(lax.broadcasted_iota(jnp.int32, s.shape, 0), steps)
        col = lax.broadcasted_iota(jnp.int32, s.shape, 1)
        w = jnp.where(col <= row, jnp.exp(s * scale), 0.0)
        dacc[r] += first_lane(w)
        acc[r] += jnp.dot(w.astype(BF), dv[j], preferred_element_type=F32)
    out[:, :, 0:128] = acc[...].astype(BF)
    den = jnp.sum(dacc[...], axis=2, keepdims=True)
    hi = den.astype(BF)
    lo = (den - hi.astype(F32)).astype(BF)
    out[:, :, 128:256] = jnp.where(lane[None] < 64, hi, lo)


def decode(req, lim, ctx, q, k, v, hk, hv, dk, dv):
    shape = q.shape
    return pl.pallas_call(
        decode_kernel,
        in_specs=[SM] * 3 + [VM] * 7,
        out_specs=VM,
        scratch_shapes=[pltpu.VMEM(shape, F32), pltpu.VMEM(shape, F32)],
        out_shape=jax.ShapeDtypeStruct((shape[0], shape[1], 256), BF),
        compiler_params=pltpu.CompilerParams(vmem_limit_bytes=16 << 20),
        cost_estimate=pl.CostEstimate(flops=10**8, bytes_accessed=3_000_000, transcendentals=10**5),
        name="decode_terms",
    )(req, lim, ctx, q, k, v, hk, hv, dk, dv)


def combine_kernel(o0, o1, o2, o3, dec, out, small):
    rows = o0.shape[0] - 16
    heads = o0.shape[1] // HD
    reqs = rows // 32
    refs = (o0, o1, o2, o3)

    def total(*at):
        t = refs[0][at].astype(F32)
        for ref in refs[1:]:
            t = t + ref[at].astype(F32)
        return t

    tail = total(pl.ds(rows, 16), pl.ds(0, 512))
    tail = tail[:, :256] + tail[:, 256:]
    den = jnp.concatenate([tail[:, :128], tail[:, 128:]], axis=0)
    for r in range(reqs):
        for h in range(heads):
            at = (pl.ds(r * 32, 32), pl.ds(h * 128, 128))
            out[at] = (total(*at) / den[:, r * 16 + h : r * 16 + h + 1]).astype(BF)
    sums = jnp.sum(dec[...].astype(F32), axis=0)
    reqs = sums.shape[0]
    dden = sums[:, :, 128:129] + sums[:, :, 192:193]
    live = lax.broadcasted_iota(jnp.int32, (1, 32, 1), 1) < heads * 4
    att = sums[:, :, :128] / jnp.where(live, dden, 1.0)
    small[...] = jnp.zeros_like(small)
    for j in range(reqs):
        for h in range(heads):
            small[j * 4 : j * 4 + 4, h * 128 : h * 128 + 128] = att[j, h * 4 : h * 4 + 4]
    out[rows : rows + 16] = small[...].astype(BF)


def combine(os, dec):
    shape = os[0].shape
    return pl.pallas_call(
        combine_kernel,
        in_specs=[VM] * 5,
        out_specs=VM,
        scratch_shapes=[pltpu.VMEM((16, shape[1]), F32)],
        out_shape=jax.ShapeDtypeStruct(shape, BF),
        compiler_params=pltpu.CompilerParams(vmem_limit_bytes=16 << 20),
        cost_estimate=pl.CostEstimate(flops=10**6, bytes_accessed=2_500_000, transcendentals=0),
        name="combine",
    )(*os, dec)


def project_kernel(at, x, w, o):
    o[...] = jnp.dot(x[...], w[...], preferred_element_type=F32)[: o.shape[0]].astype(BF)


def project_last_kernel(at, x, w, a, b, c, op, od):
    y = jnp.dot(x[...], w[...], preferred_element_type=F32)[: a.shape[0]]
    y = y + a[...].astype(F32) + b[...].astype(F32) + c[...].astype(F32)
    rows = op.shape[0]
    op[...] = y[:rows].astype(BF)
    od[...] = y[rows:].astype(BF)


def project(column, x, w, rows, parts, others=None):
    depth = x.shape[1]
    width = w.shape[1] // parts
    tile = 896
    tiles = width // tile
    xs = pl.BlockSpec(x.shape, lambda t, at: (0, 0))
    ws = pl.BlockSpec((depth, tile), lambda t, at: (0, at[0] * tiles + t))
    os = lambda n: pl.BlockSpec((n, tile), lambda t, at: (0, t))
    params = pltpu.CompilerParams(vmem_limit_bytes=32 << 20)
    cost = pl.CostEstimate(flops=2 * rows * depth * width, bytes_accessed=4_500_000, transcendentals=0)
    if others is None:
        spec = pltpu.PrefetchScalarGridSpec(
            num_scalar_prefetch=1, grid=(tiles,), in_specs=[xs, ws], out_specs=os(rows)
        )
        return pl.pallas_call(
            project_kernel, grid_spec=spec, out_shape=jax.ShapeDtypeStruct((rows, width), BF),
            compiler_params=params, cost_estimate=cost, name="project",
        )(column, x, w)
    main = rows - 8
    spec = pltpu.PrefetchScalarGridSpec(
        num_scalar_prefetch=1, grid=(tiles,), in_specs=[xs, ws] + [os(rows)] * 3, out_specs=[os(main), os(8)]
    )
    return pl.pallas_call(
        project_last_kernel, grid_spec=spec,
        out_shape=[jax.ShapeDtypeStruct((main, width), BF), jax.ShapeDtypeStruct((8, width), BF)],
        compiler_params=params, cost_estimate=cost, name="project_last",
    )(column, x, w, *others)


def sorted_tables(codes):
    index = jnp.arange(codes.shape[0], dtype=jnp.int32)
    rank = jnp.sum((codes[None, :] < codes[:, None]).astype(jnp.int32), axis=1)
    hit = rank[None, :] == index[:, None]
    order = jnp.sum(jnp.where(hit, index[None, :], 0), axis=1)
    lim = jnp.sum(jnp.where(hit, codes[None, :] & 255, 0), axis=1)
    owners = codes >> 16
    starts = jnp.sum((owners[None, :] < jnp.arange(9, dtype=jnp.int32)[:, None]).astype(jnp.int32), axis=1)
    return order, lim, starts


def visible_tokens(req, blk, bounds):
    count = bounds.shape[0]
    hit = req[:, None] == jnp.arange(count, dtype=jnp.int32)[None, :]
    bound = jnp.sum(jnp.where(hit, bounds[None, :], 0), axis=1)
    return jnp.clip(bound - blk * PAGE, 0, PAGE)


def on_device(
    p_query, p_key, p_value, p_cache_k, p_cache_v, p_slot_req, p_slot_blk, p_offsets,
    d_query, d_key, d_value, d_cache_k, d_cache_v, d_slot_req, d_slot_blk, d_lengths, out_weight,
):
    me = lax.axis_index("ctx")
    column = lax.axis_index("tp")
    ctx = lax.axis_size("ctx")
    tp = lax.axis_size("tp")

    def along_y(x, d):
        return lax.ppermute(x, "ctx", [(i, (i + 4 * d) % ctx) for i in range(ctx)])

    def across(x, bit):
        return lax.ppermute(x, "ctx", [(i, i ^ bit) for i in range(ctx)])

    def along_x(x, d):
        return lax.ppermute(x, "tp", [(i, (i + d) % tp) for i in range(tp)])

    heads = p_query.shape[3] // HD
    q0, k0, v0 = p_query[0], p_cache_k[0], p_cache_v[0]
    codes = (p_slot_req[0] * 256 + p_slot_blk[0]) * 256 + visible_tokens(
        p_slot_req[0], p_slot_blk[0], p_offsets[0]
    )
    qs = [q0, along_y(q0, 1), along_y(q0, -1), along_y(q0, 2)]
    k2, v2 = across(k0, 2), across(v0, 2)
    k1, v1 = across(k0, 1), across(v0, 1)
    span = jnp.stack([p_key[0], p_value[0]])
    spans = [span, across(span, 1), across(span, 2), across(span, 3)]
    handed = lax.ppermute(span, "sec", [(0, 1), (1, 0)])
    c1, c2, c3 = across(codes, 1), across(codes, 2), across(codes, 3)

    steps = d_query.shape[2]
    dq = d_query[0].reshape(2, steps, heads, HD).transpose(0, 2, 1, 3).reshape(2, steps * heads, HD)
    dq = jnp.pad(dq, ((0, 0), (0, 32 - steps * heads), (0, 0)))
    dq_all = lax.all_to_all(jnp.broadcast_to(dq[None], (ctx,) + dq.shape), "ctx", 0, 0)
    dq_all = dq_all.reshape(ctx * 2, 32, HD)
    pad = ((0, 0), (0, 16 - steps), (0, 0))
    dec = decode(
        d_slot_req[0],
        visible_tokens(d_slot_req[0], d_slot_blk[0], d_lengths[0]),
        me.reshape(1),
        dq_all,
        d_cache_k[0],
        d_cache_v[0],
        handed[0],
        handed[1],
        jnp.pad(d_key[0], pad),
        jnp.pad(d_value[0], pad),
    )
    dec = lax.all_to_all(dec.reshape(ctx, 2, 32, 256), "ctx", 0, 0)

    sources = jnp.stack([me, me - 4 + ctx, me + 4, me + 8]) % ctx
    bases = jnp.concatenate([sources, me ^ jnp.arange(4, dtype=jnp.int32)]).astype(jnp.int32) * 32
    joined_span = jnp.concatenate(spans, axis=2)
    near = attn(
        True, *sorted_tables(jnp.concatenate([codes, c1])), qs, (k0, k1, v0, v1),
        (bases, joined_span[0], joined_span[1]),
    )
    k3, v3 = across(k2, 1), across(v2, 1)
    o0, o1, o2, o3 = attn(False, *sorted_tables(jnp.concatenate([c2, c3])), qs, (k2, k3, v2, v3), near)
    parts = [o0, along_y(o1, -1), along_y(o2, 1), along_y(o3, 2)]
    joined = combine(parts, dec)

    rows = joined.shape[0] - 8
    share = lambda d: project(((column + d) % tp).reshape(1), joined, out_weight, rows, tp)
    far = along_x(share(2), 2)
    up = along_x(share(1), 1)
    down = along_x(share(3), -1)
    prefill_out, decode_out = project(column.reshape(1), joined, out_weight, rows, tp, (up, down, far))
    width = prefill_out.shape[1]
    return (
        prefill_out.reshape(1, p_query.shape[1], p_query.shape[2], width),
        decode_out.reshape(1, 2, steps, width),
    )


def solution(mesh):
    placed = (
        P("sec", None, "ctx", "tp"),
        P("sec", None, "ctx", "tp"),
        P("sec", None, "ctx", "tp"),
        P("sec", "ctx", None, "tp"),
        P("sec", "ctx", None, "tp"),
        P("sec", "ctx"),
        P("sec", "ctx"),
        P("sec", None),
        P("sec", "ctx", None, "tp"),
        P("sec", "ctx", None, "tp"),
        P("sec", "ctx", None, "tp"),
        P("sec", "ctx", None, "tp"),
        P("sec", "ctx", None, "tp"),
        P("sec", "ctx"),
        P("sec", "ctx"),
        P("sec", None),
        P("tp", None),
    )
    return jax.shard_map(
        on_device,
        mesh=mesh,
        in_specs=placed,
        out_specs=(P("sec", None, "ctx", "tp"), P("sec", "ctx", None, "tp")),
        check_vma=False,
    )
```

```python
import functools

import jax
import jax.numpy as jnp
from jax import lax
from jax.experimental import pallas as pl
from jax.experimental.pallas import tpu as pltpu
from jax.sharding import PartitionSpec as P

HD = 128
PAGE = 128
BF = jnp.bfloat16
F32 = jnp.float32
NT = (((1,), (1,)), ((), ()))
NB = 4
VM = pl.BlockSpec(memory_space=pltpu.VMEM)
SM = pl.BlockSpec(memory_space=pltpu.SMEM)
HBM = pl.BlockSpec(memory_space=pl.ANY)


def attn_kernel(order, lim, starts, *refs, first, r0, R, heads, half):
    rows = heads * 128
    if first:
        (bases, q0, q1, q2, q3, ka, kb, va, vb, span, num_a, num_b, qs_out, den,
         qv, qs, ks, vs, sk, num, dacc, tile, sem) = refs
    else:
        (qs_in, ka, kb, va, vb, num_in, den_in, o0, o1, o2, o3, qs, ks, vs, num, acc, dacc, sem) = refs
    cs = []

    def copy(src, dst, i):
        c = pltpu.make_async_copy(src, dst, sem.at[i])
        c.start()
        return c

    if first:
        qc = [copy(q, qv.at[d], 4 + d) for d, q in enumerate((q0, q1, q2, q3))]
        cs = [copy(span, sk, 8)]
    else:
        cs = [copy(qs_in.at[pl.ds(r0, R)], qs, 4)]
    cs += [
        copy(ka, ks.at[pl.ds(0, half)], 0),
        copy(kb, ks.at[pl.ds(half, half)], 1),
        copy(va, vs.at[pl.ds(0, half)], 2),
        copy(vb, vs.at[pl.ds(half, half)], 3),
    ]
    if not first:
        num_copy = copy(num_in, num, 5)
    if first:
        rowi = lax.broadcasted_iota(jnp.int32, (128, 128), 0)
        coli = lax.broadcasted_iota(jnp.int32, (128, 128), 1)

        def pick(i, b):
            g = i // 32
            base = jnp.where(g == 0, bases[b], jnp.where(g == 1, bases[b + 1], jnp.where(g == 2, bases[b + 2], bases[b + 3])))
            return base + lax.rem(i, 32)

        tile[...] = jnp.where(pick(rowi, 0) >= pick(coli, 4), 1.0, 0.0)
        for d in range(4):
            qc[d].wait()
            for r in range(R):
                for h in range(heads):
                    qs[r, pl.ds(h * 128 + d * 32, 32), :] = qv[d, r, :, pl.ds(h * 128, 128)]
        qs_copy = copy(qs, qs_out, 4)
    for c in cs:
        c.wait()
    lane1 = lax.broadcasted_iota(jnp.int32, (128, 128), 1)
    lane = lax.broadcasted_iota(jnp.int32, (1, 128), 1)
    if not first:
        num_copy.wait()

    def request(r, dtile):
        s0 = starts[r0 + r]
        n = starts[r0 + r + 1] - s0
        nref = num.at[r] if first else acc

        def fetch(i):
            ok = i < n
            s = jnp.where(ok, s0 + i, 0)
            b = order[s]
            return ks[b], vs[b], jnp.where(ok, lim[s], 0)

        def weights(Ks, ms):
            K = jnp.concatenate(Ks, axis=0)
            sc = lax.dot_general(qs[r], K, NT, preferred_element_type=F32)
            w = jnp.exp(sc * HD ** -0.5)
            return [m(w[:, j * 128 : (j + 1) * 128]) for j, m in enumerate(ms)]

        def keep(l):
            return lambda w: jnp.where(lane < l, w, 0.0)

        def causal(w):
            return jnp.where(tile[...][None] > 0.5, w.reshape(heads, 128, 128), 0.0).reshape(rows, 128)

        def total(ws):
            t = ws[0]
            for w in ws[1:]:
                t = t + w
            return t

        def product(ws, Vs):
            return jnp.dot(
                jnp.concatenate([w.astype(BF) for w in ws], axis=1),
                jnp.concatenate(Vs, axis=0),
                preferred_element_type=F32,
            )

        skip = 0
        if first:
            f = [fetch(i) for i in range(NB - 1)]
            ws = weights([sk[0, r]] + [x[0] for x in f], [causal] + [keep(x[2]) for x in f])
            dacc[...] = total(ws)
            nref[...] = product(ws, [sk[1, r]] + [x[1] for x in f])
            skip = NB - 1
        else:
            acc[...] = jnp.zeros_like(acc)
            dacc[...] = jnp.zeros_like(dacc)

        def step(p, unused):
            f = [fetch(skip + NB * p + i) for i in range(NB)]
            ws = weights([x[0] for x in f], [keep(x[2]) for x in f])
            dacc[...] += total(ws)
            nref[...] += product(ws, [x[1] for x in f])
            return 0

        lax.fori_loop(0, (jnp.maximum(n - skip, 0) + NB - 1) // NB, step, 0)
        upd = dtile
        for h in range(heads):
            col = jnp.sum(dacc[pl.ds(h * 128, 128), :], axis=1, keepdims=True)
            upd = upd + jnp.where(lane1 == (r0 + r) * 16 + h, col, 0.0)
        if not first:
            outs = (o0, o1, o2, o3)
            for h in range(heads):
                for d in range(4):
                    sl = pl.ds(h * 128 + d * 32, 32)
                    outs[d][pl.ds(pl.multiple_of(r * 32, 32), 32), pl.ds(h * 128, 128)] = (
                        num[r, sl, :] + acc[sl, :]
                    ).astype(BF)
        return upd

    init = jnp.zeros((128, 128), F32) if first else den_in[...]
    dl = lax.fori_loop(0, R, request, init)
    if first:
        den[...] = dl
        na = copy(num.at[pl.ds(0, R // 2)], num_a, 0)
        nb = copy(num.at[pl.ds(R // 2, R // 2)], num_b, 1)
        na.wait()
        nb.wait()
        qs_copy.wait()
    else:
        outs = (o0, o1, o2, o3)
        dl = dl[:, r0 * 16 : r0 * 16 + 64]
        hi = dl.astype(BF).astype(F32)
        both = jnp.concatenate([hi, dl - hi], axis=1).astype(BF)
        z = jnp.zeros((16, (heads - 2) * 128), BF)
        for d in range(4):
            outs[d][R * 32 : R * 32 + 16, 0:128] = both[d * 32 : d * 32 + 16]
            outs[d][R * 32 : R * 32 + 16, 128:256] = both[d * 32 + 16 : d * 32 + 32]
            outs[d][R * 32 : R * 32 + 16, 256:] = z


def attn_near(order, lim, starts, bases, qs, kv, span):
    R, T, W = qs[0].shape
    heads = W // HD
    rows = heads * 128
    nb = order.shape[0]
    body = functools.partial(attn_kernel, first=True, r0=0, R=R, heads=heads, half=nb // 2)
    return pl.pallas_call(
        body,
        in_specs=[SM] * 4 + [HBM] * 9,
        out_specs=[HBM, HBM, HBM, VM],
        scratch_shapes=[
            pltpu.VMEM((4, R, T, W), BF),
            pltpu.VMEM((R, rows, 128), BF),
            pltpu.VMEM((nb, 128, 128), BF),
            pltpu.VMEM((nb, 128, 128), BF),
            pltpu.VMEM(span.shape, BF),
            pltpu.VMEM((R, rows, 128), F32),
            pltpu.VMEM((rows, 128), F32),
            pltpu.VMEM((128, 128), F32),
            pltpu.SemaphoreType.DMA((9,)),
        ],
        out_shape=[
            jax.ShapeDtypeStruct((R // 2, rows, 128), F32),
            jax.ShapeDtypeStruct((R // 2, rows, 128), F32),
            jax.ShapeDtypeStruct((R, rows, 128), BF),
            jax.ShapeDtypeStruct((128, 128), F32),
        ],
        compiler_params=pltpu.CompilerParams(vmem_limit_bytes=48 << 20),
        cost_estimate=pl.CostEstimate(flops=4 * nb * rows * 128 * 128, bytes_accessed=12_000_000, transcendentals=nb * rows * 128),
        name="attn_near",
    )(order, lim, starts, bases, *qs, *kv, span)


def attn_far(order, lim, starts, r0, qs, kv, num, den, T, W):
    R = num.shape[0]
    heads = W // HD
    rows = heads * 128
    nb = order.shape[0]
    body = functools.partial(attn_kernel, first=False, r0=r0, R=R, heads=heads, half=nb // 2)
    return pl.pallas_call(
        body,
        in_specs=[SM] * 3 + [HBM] * 6 + [VM],
        out_specs=[VM] * 4,
        scratch_shapes=[
            pltpu.VMEM((R, rows, 128), BF),
            pltpu.VMEM((nb, 128, 128), BF),
            pltpu.VMEM((nb, 128, 128), BF),
            pltpu.VMEM((R, rows, 128), F32),
            pltpu.VMEM((rows, 128), F32),
            pltpu.VMEM((rows, 128), F32),
            pltpu.SemaphoreType.DMA((6,)),
        ],
        out_shape=[jax.ShapeDtypeStruct((R * T + 16, W), BF)] * 4,
        compiler_params=pltpu.CompilerParams(vmem_limit_bytes=48 << 20),
        cost_estimate=pl.CostEstimate(flops=2 * nb * rows * 128 * 128, bytes_accessed=12_000_000, transcendentals=nb * rows * 64),
        name="attn_far",
    )(order, lim, starts, qs, *kv, num, den)


def decode_kernel(req, lim, ctx, q, k, v, hk, hv, dk, dv, out, acc, dacc):
    scale = HD ** -0.5
    blocks = k.shape[0]
    handed = hk.shape[0]
    lane = lax.broadcasted_iota(jnp.int32, (1, 128), 1)
    acc[...] = jnp.zeros_like(acc)
    dacc[...] = jnp.zeros_like(dacc)

    def block(i, unused):
        r = req[i]
        s = lax.dot_general(q[r], k[i], NT, preferred_element_type=F32)
        w = jnp.where(lane < lim[i], jnp.exp(s * scale), 0.0)
        dacc[r] += w
        acc[r] += jnp.dot(w.astype(BF), v[i], preferred_element_type=F32)
        return 0

    lax.fori_loop(0, blocks, block, 0, unroll=True)

    def first_lane(w):
        return jnp.where(lane == 0, jnp.sum(w, axis=1, keepdims=True), 0.0)

    for r in range(handed):
        s = lax.dot_general(q[r], hk[r], NT, preferred_element_type=F32)
        w = jnp.exp(s * scale)
        dacc[r] += first_lane(w)
        acc[r] += jnp.dot(w.astype(BF), hv[r], preferred_element_type=F32)
    steps = 4
    for j in range(dk.shape[0]):
        r = ctx[0] * dk.shape[0] + j
        s = lax.dot_general(q[r], dk[j], NT, preferred_element_type=F32)
        row = lax.rem(lax.broadcasted_iota(jnp.int32, s.shape, 0), steps)
        col = lax.broadcasted_iota(jnp.int32, s.shape, 1)
        w = jnp.where(col <= row, jnp.exp(s * scale), 0.0)
        dacc[r] += first_lane(w)
        acc[r] += jnp.dot(w.astype(BF), dv[j], preferred_element_type=F32)
    out[:, :, 0:128] = acc[...].astype(BF)
    den = jnp.sum(dacc[...], axis=2, keepdims=True)
    hi = den.astype(BF)
    lo = (den - hi.astype(F32)).astype(BF)
    out[:, :, 128:256] = jnp.where(lane[None] < 64, hi, lo)


def decode(req, lim, ctx, q, k, v, hk, hv, dk, dv):
    shape = q.shape
    return pl.pallas_call(
        decode_kernel,
        in_specs=[SM] * 3 + [VM] * 7,
        out_specs=VM,
        scratch_shapes=[pltpu.VMEM(shape, F32), pltpu.VMEM(shape, F32)],
        out_shape=jax.ShapeDtypeStruct((shape[0], shape[1], 256), BF),
        compiler_params=pltpu.CompilerParams(vmem_limit_bytes=16 << 20),
        cost_estimate=pl.CostEstimate(flops=10**8, bytes_accessed=3_000_000, transcendentals=10**5),
        name="decode_terms",
    )(req, lim, ctx, q, k, v, hk, hv, dk, dv)


def combine_kernel(*refs, decode_rows):
    if decode_rows:
        o0, o1, o2, o3, dec, out, small = refs
    else:
        o0, o1, o2, o3, out = refs
    rows = o0.shape[0] - 16
    heads = o0.shape[1] // HD
    parts = (o0, o1, o2, o3)

    def total(*at):
        t = parts[0][at].astype(F32)
        for ref in parts[1:]:
            t = t + ref[at].astype(F32)
        return t

    tail = total(pl.ds(rows, 16), pl.ds(0, 256))
    den = jnp.concatenate([tail[:, :128], tail[:, 128:]], axis=0)
    den = den[:, :64] + den[:, 64:]
    for r in range(rows // 32):
        for h in range(heads):
            at = (pl.ds(r * 32, 32), pl.ds(h * 128, 128))
            out[at] = (total(*at) / den[:, r * 16 + h : r * 16 + h + 1]).astype(BF)
    if not decode_rows:
        return
    sums = jnp.sum(dec[...].astype(F32), axis=0)
    reqs = sums.shape[0]
    dden = sums[:, :, 128:129] + sums[:, :, 192:193]
    att = sums[:, :, :128] / dden
    small[...] = jnp.zeros_like(small)
    for j in range(reqs):
        for h in range(heads):
            small[j * 4 : j * 4 + 4, h * 128 : h * 128 + 128] = att[j, h * 4 : h * 4 + 4]
    out[rows : rows + 16] = small[...].astype(BF)


def combine(os, dec=None):
    rows, width = os[0].shape
    more = [] if dec is None else [dec]
    out_rows = rows if more else rows - 16
    return pl.pallas_call(
        functools.partial(combine_kernel, decode_rows=len(more)),
        in_specs=[VM] * (4 + len(more)),
        out_specs=VM,
        scratch_shapes=[pltpu.VMEM((16, width), F32)] * len(more),
        out_shape=jax.ShapeDtypeStruct((out_rows, width), BF),
        compiler_params=pltpu.CompilerParams(vmem_limit_bytes=16 << 20),
        cost_estimate=pl.CostEstimate(flops=10**6, bytes_accessed=2_500_000, transcendentals=0),
        name="combine",
    )(*os, *more)


def project_kernel(own, other, x0, x1, x2, x3, w0, a1, a2, a3, b1, b2, b3, *outs):
    def run(ws):
        y = jnp.dot(x0[...], w0[...], preferred_element_type=F32)
        for x, w in zip((x1, x2, x3), ws):
            y = y + jnp.dot(x[...], w[...], preferred_element_type=F32)
        rows = outs[0].shape[0]
        outs[0][...] = y[:rows].astype(BF)
        if len(outs) > 1:
            outs[1][...] = y[rows : rows + outs[1].shape[0]].astype(BF)

    @pl.when(pl.program_id(0) == 0)
    def _():
        run((a1, a2, a3))

    @pl.when(pl.program_id(0) == 1)
    def _():
        run((b1, b2, b3))


def project(own, other, xs, w, mine, theirs, small):
    rows, depth = xs[0].shape
    half = mine[0].shape[1]
    full = lambda a: pl.BlockSpec(a.shape, lambda t, o, q: (0, 0))
    side = lambda t, o, q: jnp.where(t == 0, o[0], q[0])
    main = rows - (16 if small else 0)
    shapes = [jax.ShapeDtypeStruct((main, 2 * half), BF)]
    out_specs = [pl.BlockSpec((main, half), lambda t, o, q: (0, lax.rem(side(t, o, q), 2)))]
    if small:
        shapes.append(jax.ShapeDtypeStruct((small, 2 * half), BF))
        out_specs.append(pl.BlockSpec((small, half), lambda t, o, q: (0, lax.rem(side(t, o, q), 2))))
    spec = pltpu.PrefetchScalarGridSpec(
        num_scalar_prefetch=2,
        grid=(2,),
        in_specs=[full(x) for x in xs]
        + [pl.BlockSpec((depth, half), lambda t, o, q: (0, side(t, o, q)))]
        + [full(a) for a in mine + theirs],
        out_specs=out_specs,
    )
    return pl.pallas_call(
        project_kernel,
        grid_spec=spec,
        out_shape=shapes,
        compiler_params=pltpu.CompilerParams(vmem_limit_bytes=48 << 20),
        cost_estimate=pl.CostEstimate(flops=8 * rows * depth * 2 * half, bytes_accessed=14_000_000, transcendentals=0),
        name="project",
    )(own, other, *xs, w, *mine, *theirs)


def sorted_tables(req, lim):
    index = jnp.arange(req.shape[0], dtype=jnp.int32)
    key = req * 256 + index
    rank = jnp.sum((key[None, :] < key[:, None]).astype(jnp.int32), axis=1)
    hit = rank[None, :] == index[:, None]
    order = jnp.sum(jnp.where(hit, index[None, :], 0), axis=1)
    lims = jnp.sum(jnp.where(hit, lim[None, :], 0), axis=1)
    starts = jnp.sum((req[None, :] < jnp.arange(9, dtype=jnp.int32)[:, None]).astype(jnp.int32), axis=1)
    return order, lims, starts


def visible_tokens(req, blk, bounds):
    count = bounds.shape[0]
    hit = req[:, None] == jnp.arange(count, dtype=jnp.int32)[None, :]
    bound = jnp.sum(jnp.where(hit, bounds[None, :], 0), axis=1)
    return jnp.clip(bound - blk * PAGE, 0, PAGE)


def on_device(
    p_query, p_key, p_value, p_cache_k, p_cache_v, p_slot_req, p_slot_blk, p_offsets,
    d_query, d_key, d_value, d_cache_k, d_cache_v, d_slot_req, d_slot_blk, d_lengths, out_weight,
):
    me = lax.axis_index("ctx")
    column = lax.axis_index("tp")
    core = me % 2
    ctx = lax.axis_size("ctx")
    tp = lax.axis_size("tp")

    def along_y(x, d):
        return lax.ppermute(x, "ctx", [(i, (i + 4 * d) % ctx) for i in range(ctx)])

    def across(x, bit):
        return lax.ppermute(x, "ctx", [(i, i ^ bit) for i in range(ctx)])

    def along_x(x, d):
        return lax.ppermute(x, "tp", [(i, (i + d) % tp) for i in range(tp)])

    heads = p_query.shape[3] // HD
    reqs, span_len = p_query.shape[1:3]
    slots = p_slot_req.shape[1]
    steps = d_query.shape[2]
    width = heads * HD
    q0, k0, v0 = p_query[0], p_cache_k[0], p_cache_v[0]

    k2, v2 = across(k0, 2), across(v0, 2)
    k1, v1 = across(k0, 1), across(v0, 1)
    qs = [q0, along_y(q0, 1), along_y(q0, -1), along_y(q0, 2)]
    lim0 = visible_tokens(p_slot_req[0], p_slot_blk[0], p_offsets[0])
    table = jnp.pad(jnp.stack([p_slot_req[0], lim0]), ((0, 14), (0, HD - slots))).astype(BF)
    note = jnp.concatenate(
        [p_key[0].reshape(-1, HD), p_value[0].reshape(-1, HD), table], axis=0
    )
    notes = [note, across(note, 1), across(note, 2), across(note, 3)]
    handed = lax.ppermute(note, "sec", [(0, 1), (1, 0)])[: 2 * reqs * span_len]
    handed = handed.reshape(2, reqs, span_len, HD)
    spans = [n[: 2 * reqs * span_len].reshape(2, reqs, span_len, HD) for n in notes]
    reqs_of = [n[2 * reqs * span_len, :slots].astype(jnp.int32) for n in notes]
    lims_of = [n[2 * reqs * span_len + 1, :slots].astype(jnp.int32) for n in notes]

    half = out_weight.shape[1] // (2 * tp)
    block = lambda d: lax.dynamic_slice(
        out_weight, (0, (((column + d) % tp) * 2 + core) * half), (out_weight.shape[0], half)
    )
    mine = [along_x(block(1), 1), along_x(block(3), -1), along_x(block(2), 2)]
    theirs = [across(w, 1) for w in mine]

    dq = d_query[0].reshape(2, steps, heads, HD).transpose(0, 2, 1, 3).reshape(2, steps * heads, HD)
    dq = jnp.pad(dq, ((0, 0), (0, 32 - steps * heads), (0, 0)))
    dq_all = lax.all_to_all(jnp.broadcast_to(dq[None], (ctx,) + dq.shape), "ctx", 0, 0)
    dq_all = dq_all.reshape(ctx * 2, 32, HD)
    pad = ((0, 0), (0, 16 - steps), (0, 0))
    dec = decode(
        d_slot_req[0],
        visible_tokens(d_slot_req[0], d_slot_blk[0], d_lengths[0]),
        me.reshape(1),
        dq_all,
        d_cache_k[0],
        d_cache_v[0],
        handed[0],
        handed[1],
        jnp.pad(d_key[0], pad),
        jnp.pad(d_value[0], pad),
    )
    dec = lax.all_to_all(dec.reshape(ctx, 2, 32, 256), "ctx", 0, 0)

    sources = jnp.stack([me, me - 4 + ctx, me + 4, me + 8]) % ctx
    bases = jnp.concatenate([sources, me ^ jnp.arange(4, dtype=jnp.int32)]).astype(jnp.int32) * span_len
    near_tables = sorted_tables(jnp.concatenate(reqs_of[:2]), jnp.concatenate(lims_of[:2]))
    far_tables = sorted_tables(jnp.concatenate(reqs_of[2:]), jnp.concatenate(lims_of[2:]))
    num_a, num_b, queries, den = attn_near(
        *near_tables, bases, qs, (k0, k1, v0, v1), jnp.concatenate(spans, axis=2)
    )
    k2, v2, num_a, num_b, queries, den = lax.optimization_barrier((k2, v2, num_a, num_b, queries, den))
    k3, v3 = across(k2, 1), across(v2, 1)
    kv = (k2, k3, v2, v3)
    oa = attn_far(*far_tables, 0, queries, kv, num_a, den, span_len, width)
    sent_a = [oa[0], along_y(oa[1], -1), along_y(oa[2], 1), along_y(oa[3], 2)]
    ob = attn_far(*far_tables, reqs // 2, queries, kv, num_b, den, span_len, width)
    sent_b = [ob[0], along_y(ob[1], -1), along_y(ob[2], 1), along_y(ob[3], 2)]

    def gathered(x):
        return [x, along_x(x, 1), along_x(x, -1), along_x(x, 2)]

    xa = gathered(combine(sent_a, dec))
    xb = gathered(combine(sent_b))
    own = (column * 2 + core).reshape(1)
    other = (column * 2 + 1 - core).reshape(1)
    pa, decode_out = project(own, other, xa, out_weight, mine, theirs, 2 * steps)
    (pb,) = project(own, other, xb, out_weight, mine, theirs, 0)
    width = pa.shape[1]
    prefill_out = jnp.concatenate(
        [p.reshape(1, reqs // 2, span_len, width) for p in (pa, pb)], axis=1
    )
    return prefill_out, decode_out.reshape(1, 2, steps, width)


def solution(mesh):
    placed = (
        P("sec", None, "ctx", "tp"),
        P("sec", None, "ctx", "tp"),
        P("sec", None, "ctx", "tp"),
        P("sec", "ctx", None, "tp"),
        P("sec", "ctx", None, "tp"),
        P("sec", "ctx"),
        P("sec", "ctx"),
        P("sec", None),
        P("sec", "ctx", None, "tp"),
        P("sec", "ctx", None, "tp"),
        P("sec", "ctx", None, "tp"),
        P("sec", "ctx", None, "tp"),
        P("sec", "ctx", None, "tp"),
        P("sec", "ctx"),
        P("sec", "ctx"),
        P("sec", None),
        P("tp", None),
    )
    return jax.shard_map(
        on_device,
        mesh=mesh,
        in_specs=placed,
        out_specs=(P("sec", None, "ctx", "tp"), P("sec", "ctx", None, "tp")),
        check_vma=False,
    )
```

```python
import functools

import jax
import jax.numpy as jnp
from jax import lax
from jax.experimental import pallas as pl
from jax.experimental.pallas import tpu as pltpu
from jax.sharding import PartitionSpec as P

HD = 128
PAGE = 128
BF = jnp.bfloat16
F32 = jnp.float32
NT = (((1,), (1,)), ((), ()))
VM = pl.BlockSpec(memory_space=pltpu.VMEM)
SM = pl.BlockSpec(memory_space=pltpu.SMEM)
HBM = pl.BlockSpec(memory_space=pl.ANY)


def attn_kernel(table, *refs, first, r0, R, heads, nb):
    rows = heads * 128
    half = nb // 2
    if first:
        rel, q_all, ma, mb, num_out, qs_out, den, qv, qs, ks, vs, acc, dacc, p0, p1, sem = refs
    else:
        (bases, qs_in, ma, mb, mc, md, num_in, den_in, o0, o1, o2, o3,
         qs, ks, vs, acc, dacc, p0, p1, tile, sem) = refs
    cs = []

    def copy(src, dst, i):
        c = pltpu.make_async_copy(src, dst, sem.at[i])
        c.start()
        return c

    if first:
        qc = [copy(q_all.at[rel[d]], qv.at[d], 4 + d) for d in range(4)]
        sets = (ma, mb)
    else:
        cs = [copy(qs_in.at[pl.ds(r0, R)], qs, 4), copy(num_in.at[pl.ds(r0, R)], acc, 5)]
        sets = (mc, md)
    for i, m in enumerate(sets):
        cs.append(copy(m.at[pl.ds(0, half)], ks.at[pl.ds(i * half, half)], 2 * i))
        cs.append(copy(m.at[pl.ds(half, half)], vs.at[pl.ds(i * half, half)], 2 * i + 1))
    if not first:
        for i, m in enumerate((ma, mb, mc, md)):
            for j, dst in enumerate((ks, vs)):
                for r in range(R):
                    at = nb + j * 2 + (r0 + r) // 4
                    c = pltpu.make_async_copy(
                        m.at[at, pl.ds((r0 + r) % 4 * 32, 32)],
                        dst.at[nb + r, pl.ds(i * 32, 32)],
                        sem.at[6 + (i * 2 + j) * R + r],
                    )
                    c.start()
                    cs.append(c)
    dacc[...] = jnp.zeros_like(dacc)
    p1[...] = jnp.zeros_like(p1)
    if first:
        acc[...] = jnp.zeros_like(acc)
        for d in range(4):
            qc[d].wait()
            for r in range(R):
                for h in range(heads):
                    qs[r, pl.ds(h * 128 + d * 32, 32), :] = qv[d, r, :, pl.ds(h * 128, 128)]
        qs_copy = copy(qs, qs_out, 4)
    else:
        rowi = lax.broadcasted_iota(jnp.int32, (128, 128), 0)
        coli = lax.broadcasted_iota(jnp.int32, (128, 128), 1)

        def pick(i, b):
            g = i // 32
            base = jnp.where(
                g == 0, bases[b], jnp.where(g == 1, bases[b + 1], jnp.where(g == 2, bases[b + 2], bases[b + 3]))
            )
            return base + lax.rem(i, 32)

        tile[...] = jnp.where(pick(rowi, 0) >= pick(coli, 4), coli + 1, 0)
    for c in cs:
        c.wait()
    lane = lax.broadcasted_iota(jnp.int32, (1, 128), 1)
    begin, end = table[3, r0], table[3, r0 + R]

    def pair(p):
        ok = jnp.logical_and(p >= begin, p < end)
        i = jnp.where(ok, 2 * p, 0)
        r = jnp.where(ok, table[2, jnp.where(ok, p, 0)] - r0, 0)
        slots = table[0, i], table[0, i + 1]
        lims = jnp.where(ok, table[1, i], 0), jnp.where(ok, table[1, i + 1], 0)
        return r, slots, lims

    def scores(p, dst):
        r, slots, lims = pair(p)
        if not first:
            slots = [jnp.where(l == 200, nb + r, s) for s, l in zip(slots, lims)]
        K = jnp.concatenate([ks[slots[0]], ks[slots[1]]], axis=0)
        s = lax.dot_general(qs[r], K, NT, preferred_element_type=F32)
        w = jnp.exp(s * HD ** -0.5)
        t = None
        for j in range(2):
            limit = lims[j]
            if first or j:
                keep = (lane < limit)[None]
            else:
                keep = (lane < jnp.where(limit == 200, tile[...], limit))[None]
            one = w[:, j * 128 : (j + 1) * 128].reshape(heads, 128, 128)
            one = jnp.where(keep, one, 0.0).reshape(rows, 128)
            dst[:, j * 128 : (j + 1) * 128] = one.astype(BF)
            t = one if t is None else t + one
        dacc[r] += t

    def products(p, src):
        r, slots, lims = pair(p)
        if not first:
            slots = [jnp.where(l == 200, nb + r, s) for s, l in zip(slots, lims)]
        V = jnp.concatenate([vs[slots[0]], vs[slots[1]]], axis=0)
        acc[r] += jnp.dot(src[...], V, preferred_element_type=F32)

    def step(i, unused):
        p = begin + 2 * i
        products(p - 1, p1)
        scores(p, p0)
        products(p, p0)
        scores(p + 1, p1)
        return 0

    steps = (end - begin + 1) // 2
    lax.fori_loop(0, steps, step, 0)
    products(begin + 2 * steps - 1, p1)

    lane1 = lax.broadcasted_iota(jnp.int32, (128, 128), 1)
    dl = jnp.zeros((128, 128), F32) if first else den_in[...]
    if first:
        num_copy = copy(acc, num_out, 0)
    for r in range(R):
        for h in range(heads):
            col = jnp.sum(dacc[r, pl.ds(h * 128, 128), :], axis=1, keepdims=True)
            dl = dl + jnp.where(lane1 == (r0 + r) * 16 + h, col, 0.0)
    if first:
        den[...] = dl
        num_copy.wait()
        qs_copy.wait()
        return
    outs = (o0, o1, o2, o3)
    for r in range(R):
        for h in range(heads):
            for d in range(4):
                outs[d][r * 32 : r * 32 + 32, h * 128 : h * 128 + 128] = acc[
                    r, h * 128 + d * 32 : h * 128 + d * 32 + 32, :
                ].astype(BF)
    dl = dl[:, r0 * 16 : r0 * 16 + 64]
    hi = dl.astype(BF).astype(F32)
    both = jnp.concatenate([hi, dl - hi], axis=1).astype(BF)
    z = jnp.zeros((16, (heads - 2) * 128), BF)
    for d in range(4):
        outs[d][R * 32 : R * 32 + 16, 0:128] = both[d * 32 : d * 32 + 16]
        outs[d][R * 32 : R * 32 + 16, 128:256] = both[d * 32 + 16 : d * 32 + 32]
        outs[d][R * 32 : R * 32 + 16, 256:] = z


def attn_near(table, rel, qs, sets, slots):
    R, T, W = qs.shape[1:]
    heads = W // HD
    rows = heads * 128
    nb = 2 * slots
    body = functools.partial(attn_kernel, first=True, r0=0, R=R, heads=heads, nb=nb)
    return pl.pallas_call(
        body,
        in_specs=[SM] * 2 + [HBM] * 3,
        out_specs=[HBM, HBM, VM],
        scratch_shapes=[
            pltpu.VMEM((4, R, T, W), BF),
            pltpu.VMEM((R, rows, 128), BF),
            pltpu.VMEM((nb, 128, 128), BF),
            pltpu.VMEM((nb, 128, 128), BF),
            pltpu.VMEM((R, rows, 128), F32),
            pltpu.VMEM((R, rows, 128), F32),
            pltpu.VMEM((rows, 256), BF),
            pltpu.VMEM((rows, 256), BF),
            pltpu.SemaphoreType.DMA((8,)),
        ],
        out_shape=[
            jax.ShapeDtypeStruct((R, rows, 128), F32),
            jax.ShapeDtypeStruct((R, rows, 128), BF),
            jax.ShapeDtypeStruct((128, 128), F32),
        ],
        compiler_params=pltpu.CompilerParams(vmem_limit_bytes=48 << 20),
        cost_estimate=pl.CostEstimate(
            flops=4 * nb * rows * 128 * 128, bytes_accessed=12_000_000, transcendentals=nb * rows * 128
        ),
        name="attn_near",
    )(table, rel, qs, *sets)


def attn_far(table, bases, r0, R, qs, sets, slots, num, den, T, W):
    heads = W // HD
    rows = heads * 128
    nb = 2 * slots
    body = functools.partial(attn_kernel, first=False, r0=r0, R=R, heads=heads, nb=nb)
    return pl.pallas_call(
        body,
        in_specs=[SM] * 2 + [HBM] * 6 + [VM],
        out_specs=[VM] * 4,
        scratch_shapes=[
            pltpu.VMEM((R, rows, 128), BF),
            pltpu.VMEM((nb + R, 128, 128), BF),
            pltpu.VMEM((nb + R, 128, 128), BF),
            pltpu.VMEM((R, rows, 128), F32),
            pltpu.VMEM((R, rows, 128), F32),
            pltpu.VMEM((rows, 256), BF),
            pltpu.VMEM((rows, 256), BF),
            pltpu.VMEM((128, 128), jnp.int32),
            pltpu.SemaphoreType.DMA((6 + 8 * R,)),
        ],
        out_shape=[jax.ShapeDtypeStruct((R * T + 16, W), BF)] * 4,
        compiler_params=pltpu.CompilerParams(vmem_limit_bytes=48 << 20),
        cost_estimate=pl.CostEstimate(
            flops=2 * nb * rows * 128 * 128, bytes_accessed=12_000_000, transcendentals=nb * rows * 64
        ),
        name="attn_far",
    )(table, bases, qs, *sets, num, den)


def pair_table(req, lim, slot, count):
    n = req.shape[0]
    size = n + count + 2
    places = jnp.arange(size, dtype=jnp.int32)
    ids = jnp.arange(count + 1, dtype=jnp.int32)
    index = jnp.arange(n, dtype=jnp.int32)
    counts = jnp.sum((req[None, :] == ids[:, None]).astype(jnp.int32), axis=1)
    pairs = (counts + 1) // 2
    first = jnp.sum(jnp.where(ids[None, :] < ids[:, None], pairs[None, :], 0), axis=1)
    before = jnp.logical_and(req[None, :] == req[:, None], index[None, :] < index[:, None])
    rank = jnp.sum(before.astype(jnp.int32), axis=1)
    base = jnp.sum(jnp.where(req[:, None] == ids[None, :], first[None, :], 0), axis=1)
    place = 2 * base + rank
    hit = place[None, :] == places[:, None]
    slots = jnp.sum(jnp.where(hit, slot[None, :], 0), axis=1)
    lims = jnp.sum(jnp.where(hit, lim[None, :], 0), axis=1)
    owner = jnp.sum((first[None, 1:] <= places[:, None]).astype(jnp.int32), axis=1)
    owner = jnp.minimum(owner, count - 1)
    firsts = jnp.pad(first, (0, size - count - 1))
    return jnp.stack([slots, lims, owner, firsts])


def decode_kernel(req, lim, ctx, q, k_hbm, v_hbm, hand, dk, dv, out, k, v, acc, dacc, sem):
    k_copy = pltpu.make_async_copy(k_hbm, k, sem.at[0])
    v_copy = pltpu.make_async_copy(v_hbm, v, sem.at[1])
    k_copy.start()
    v_copy.start()
    scale = HD ** -0.5
    blocks = k.shape[0]
    handed = hand.shape[1]
    lane = lax.broadcasted_iota(jnp.int32, (1, 128), 1)
    acc[...] = jnp.zeros_like(acc)
    dacc[...] = jnp.zeros_like(dacc)
    k_copy.wait()
    v_copy.wait()

    def block(i, unused):
        r = req[i]
        s = lax.dot_general(q[r], k[i], NT, preferred_element_type=F32)
        w = jnp.where(lane < lim[i], jnp.exp(s * scale), 0.0)
        dacc[r] += w
        acc[r] += jnp.dot(w.astype(BF), v[i], preferred_element_type=F32)
        return 0

    lax.fori_loop(0, blocks, block, 0, unroll=True)

    def first_lane(w):
        return jnp.where(lane == 0, jnp.sum(w, axis=1, keepdims=True), 0.0)

    for r in range(handed):
        s = lax.dot_general(q[r], hand[0, r], NT, preferred_element_type=F32)
        w = jnp.exp(s * scale)
        dacc[r] += first_lane(w)
        acc[r] += jnp.dot(w.astype(BF), hand[1, r], preferred_element_type=F32)
    steps = 4
    for j in range(dk.shape[0]):
        r = ctx[0] * dk.shape[0] + j
        s = lax.dot_general(q[r], dk[j], NT, preferred_element_type=F32)
        row = lax.rem(lax.broadcasted_iota(jnp.int32, s.shape, 0), steps)
        col = lax.broadcasted_iota(jnp.int32, s.shape, 1)
        w = jnp.where(col <= row, jnp.exp(s * scale), 0.0)
        dacc[r] += first_lane(w)
        acc[r] += jnp.dot(w.astype(BF), dv[j], preferred_element_type=F32)
    out[:, :, 0:128] = acc[...].astype(BF)
    den = jnp.sum(dacc[...], axis=2, keepdims=True)
    hi = den.astype(BF)
    lo = (den - hi.astype(F32)).astype(BF)
    out[:, :, 128:256] = jnp.where(lane[None] < 64, hi, lo)


def decode(req, lim, ctx, q, k, v, hand, dk, dv):
    shape = q.shape
    return pl.pallas_call(
        decode_kernel,
        in_specs=[SM] * 3 + [VM] + [HBM] * 2 + [VM] * 3,
        out_specs=VM,
        scratch_shapes=[pltpu.VMEM(k.shape, BF), pltpu.VMEM(v.shape, BF), pltpu.VMEM(shape, F32), pltpu.VMEM(shape, F32), pltpu.SemaphoreType.DMA((2,))],
        out_shape=jax.ShapeDtypeStruct((shape[0], shape[1], 256), BF),
        compiler_params=pltpu.CompilerParams(vmem_limit_bytes=16 << 20),
        cost_estimate=pl.CostEstimate(flops=10**8, bytes_accessed=3_000_000, transcendentals=10**5),
        name="decode_terms",
    )(req, lim, ctx, q, k, v, hand, dk, dv)


def combine_kernel(*refs, decode_rows):
    if decode_rows:
        h0, h1, h2, h3, dec, out, parts, small, sem = refs
    else:
        h0, h1, h2, h3, out, parts, sem = refs
    copies = [pltpu.make_async_copy(h, parts.at[i], sem.at[i]) for i, h in enumerate((h0, h1, h2, h3))]
    for c in copies:
        c.start()
    rows = parts.shape[1] - 16
    heads = parts.shape[2] // HD
    if decode_rows:
        sums = jnp.sum(dec[...].astype(F32), axis=0)
        reqs = sums.shape[0]
        dden = sums[:, :, 128:129] + sums[:, :, 192:193]
        att = sums[:, :, :128] / dden
        small[...] = jnp.zeros_like(small)
        for j in range(reqs):
            for h in range(heads):
                small[j * 4 : j * 4 + 4, h * 128 : h * 128 + 128] = att[j, h * 4 : h * 4 + 4]
        out[rows : rows + small.shape[0]] = small[...].astype(BF)
    for c in copies:
        c.wait()

    def total(*at):
        t = parts[(0,) + at].astype(F32)
        for i in range(1, 4):
            t = t + parts[(i,) + at].astype(F32)
        return t

    tail = total(pl.ds(rows, 16), pl.ds(0, 256))
    den = jnp.concatenate([tail[:, :128], tail[:, 128:]], axis=0)
    inv = 1.0 / (den[:, :64] + den[:, 64:])
    for r in range(rows // 32):
        for h in range(heads):
            at = (pl.ds(r * 32, 32), pl.ds(h * 128, 128))
            out[at] = (total(*at) * inv[:, r * 16 + h : r * 16 + h + 1]).astype(BF)


def combine(os, dec=None):
    rows, width = os[0].shape
    more = [] if dec is None else [dec]
    out_rows = rows + 16 if more else rows - 16
    return pl.pallas_call(
        functools.partial(combine_kernel, decode_rows=len(more)),
        in_specs=[HBM] * 4 + [VM] * len(more),
        out_specs=VM,
        scratch_shapes=[pltpu.VMEM((4, rows, width), BF)]
        + [pltpu.VMEM((32, width), F32)] * len(more)
        + [pltpu.SemaphoreType.DMA((4,))],
        out_shape=jax.ShapeDtypeStruct((out_rows, width), BF),
        compiler_params=pltpu.CompilerParams(vmem_limit_bytes=24 << 20),
        cost_estimate=pl.CostEstimate(flops=10**6, bytes_accessed=2_500_000, transcendentals=0),
        name="combine",
    )(*os, *more)


def project_kernel(at, *refs, row0, gathered):
    if gathered:
        x, refs = refs[0], refs[1:]
        xs = [x.at[at[3 + d]] for d in range(4)]
    else:
        xs, refs = refs[:4], refs[4:]
    w, a1, a2, a3, b1, b2, b3 = refs[:7]
    refs = refs[7:]
    if row0 == 0:
        out, small, ws, stage, sem = refs
    else:
        _, out, ws, stage, sem = refs
    half = stage.shape[2]
    rows = stage.shape[1]
    copies = []
    for t, got in enumerate(((a1, a2, a3), (b1, b2, b3))):
        col = pl.multiple_of(at[t] * half, half)
        for d, part in enumerate([w.at[:, pl.ds(col, half)]] + list(got)):
            c = pltpu.make_async_copy(part, ws.at[t * 4 + d], sem.at[t * 4 + d])
            c.start()
            copies.append(c)
    outs = []
    for t in range(2):
        y = None
        for d in range(4):
            copies[t * 4 + d].wait()
            one = jnp.dot(xs[d][...], ws[t * 4 + d], preferred_element_type=F32)
            y = one if y is None else y + one
        side = at[2] if t == 0 else 1 - at[2]
        cols = pl.ds(pl.multiple_of(side * half, half), half)
        stage[t] = y[:rows].astype(BF)
        if row0 == 0:
            small[:, cols] = y[rows : rows + 16].astype(BF)
        c = pltpu.make_async_copy(stage.at[t], out.at[pl.ds(row0, rows), cols], sem.at[8 + t])
        c.start()
        outs.append(c)
    for c in outs:
        c.wait()


def project(at, xs, w, mine, theirs, total, out=None):
    rows, depth = xs[0].shape[-2:]
    half = mine[0].shape[1]
    first = out is None
    rows = rows - (32 if first else 0)
    row0 = 0 if first else total - rows
    shape = jax.ShapeDtypeStruct((total, 2 * half), BF)
    more = [] if first else [out]
    return pl.pallas_call(
        functools.partial(project_kernel, row0=row0, gathered=len(xs) == 1),
        in_specs=[SM] + [VM] * len(xs) + [HBM] * (7 + len(more)),
        out_specs=[HBM, VM] if first else HBM,
        out_shape=[shape, jax.ShapeDtypeStruct((16, 2 * half), BF)] if first else shape,
        scratch_shapes=[
            pltpu.VMEM((8, depth, half), BF),
            pltpu.VMEM((2, rows, half), BF),
            pltpu.SemaphoreType.DMA((10,)),
        ],
        input_output_aliases={} if first else {8 + len(xs): 0},
        compiler_params=pltpu.CompilerParams(vmem_limit_bytes=48 << 20),
        cost_estimate=pl.CostEstimate(
            flops=16 * rows * depth * half, bytes_accessed=14_000_000, transcendentals=0
        ),
        name="project",
    )(at, *xs, w, *mine, *theirs, *more)


def visible_tokens(req, blk, bounds):
    count = bounds.shape[0]
    hit = req[:, None] == jnp.arange(count, dtype=jnp.int32)[None, :]
    bound = jnp.sum(jnp.where(hit, bounds[None, :], 0), axis=1)
    return jnp.clip(bound - blk * PAGE, 0, PAGE)


def on_device(
    p_query, p_key, p_value, p_cache_k, p_cache_v, p_slot_req, p_slot_blk, p_offsets,
    d_query, d_key, d_value, d_cache_k, d_cache_v, d_slot_req, d_slot_blk, d_lengths, out_weight,
):
    me = lax.axis_index("ctx")
    column = lax.axis_index("tp")
    core = me % 2
    ctx = lax.axis_size("ctx")
    tp = lax.axis_size("tp")

    def along_y(x, d):
        return lax.ppermute(x, "ctx", [(i, (i + 4 * d) % ctx) for i in range(ctx)])

    def across(x, bit):
        return lax.ppermute(x, "ctx", [(i, i ^ bit) for i in range(ctx)])

    def along_x(x, d):
        return lax.ppermute(x, "tp", [(i, (i + d) % tp) for i in range(tp)])

    heads = p_query.shape[3] // HD
    reqs, span_len = p_query.shape[1:3]
    slots = p_slot_req.shape[1]
    steps = d_query.shape[2]
    width = heads * HD

    rings = [[z + 4 * y for y in range(ctx // 4)] for z in range(4)]
    qs = lax.all_gather(p_query, "ctx", axis_index_groups=rings, tiled=True)
    span = jnp.concatenate([p_key[0].reshape(-1, PAGE, HD), p_value[0].reshape(-1, PAGE, HD)], axis=0)
    m0 = jnp.concatenate([p_cache_k[0], p_cache_v[0], span], axis=0)
    half = out_weight.shape[1] // (2 * tp)
    block = lambda d: lax.dynamic_slice(
        out_weight, (0, (((column + d) % tp) * 2 + core) * half), (out_weight.shape[0], half)
    )
    m0, w1, w3, p_slot_req, d_query, span = lax.optimization_barrier(
        (m0, block(1), block(3), p_slot_req, d_query, span)
    )
    m2 = across(m0, 2)
    w1, w3 = along_x(w1, 1), along_x(w3, -1)
    m1 = across(m0, 1)

    lim0 = visible_tokens(p_slot_req[0], p_slot_blk[0], p_offsets[0])
    note = jnp.pad(jnp.stack([p_slot_req[0], lim0]), ((0, 6), (0, HD - slots)))
    notes = [note, across(note, 1), across(note, 2), across(note, 3)]
    handed = lax.ppermute(span, "sec", [(0, 1), (1, 0)]).reshape(2, reqs, span_len, HD)

    dq = d_query[0].reshape(2, steps, heads, HD).transpose(0, 2, 1, 3).reshape(2, steps * heads, HD)
    dq = jnp.pad(dq, ((0, 0), (0, 32 - steps * heads), (0, 0)))
    dq_all = lax.all_to_all(jnp.broadcast_to(dq[None], (ctx,) + dq.shape), "ctx", 0, 0)

    index = jnp.arange(slots, dtype=jnp.int32)
    ids = jnp.arange(reqs, dtype=jnp.int32)
    near_table = pair_table(
        jnp.concatenate([n[0, :slots] for n in notes[:2]]),
        jnp.concatenate([n[1, :slots] for n in notes[:2]]),
        jnp.concatenate([index, index + slots]),
        reqs,
    )
    far_table = pair_table(
        jnp.concatenate([ids] + [n[0, :slots] for n in notes[2:]]),
        jnp.concatenate([jnp.full_like(ids, 200)] + [n[1, :slots] for n in notes[2:]]),
        jnp.concatenate([jnp.zeros_like(ids), index, index + slots]),
        reqs,
    )
    ring = (me // 4 + jnp.array([0, 3, 1, 2], dtype=jnp.int32)) % (ctx // 4)
    bases = jnp.concatenate([ring * 4 + me % 4, me ^ jnp.arange(4, dtype=jnp.int32)]).astype(jnp.int32) * span_len

    num, queries, den = attn_near(near_table, ring.astype(jnp.int32), qs, (m0, m1), slots)
    m2, w1, w3, out_weight, num, queries, den, dq_all, handed = lax.optimization_barrier(
        (m2, w1, w3, out_weight, num, queries, den, dq_all, handed)
    )
    m3 = across(m2, 1)
    w2 = along_x(
        lax.dynamic_slice(out_weight, (0, (((column + 2) % tp) * 2 + core) * half), (out_weight.shape[0], half)), 2
    )
    pad = ((0, 0), (0, 16 - steps), (0, 0))
    dec = decode(
        d_slot_req[0],
        visible_tokens(d_slot_req[0], d_slot_blk[0], d_lengths[0]),
        me.reshape(1),
        dq_all.reshape(ctx * 2, 32, HD),
        d_cache_k[0],
        d_cache_v[0],
        handed,
        jnp.pad(d_key[0], pad),
        jnp.pad(d_value[0], pad),
    )
    dec, far_table = lax.optimization_barrier((dec, far_table))
    dec = lax.all_to_all(dec.reshape(ctx, 2, 32, 256), "ctx", 0, 0)
    sets = (m0, m1, m2, m3)
    hr = reqs // 2
    oa = attn_far(far_table, bases, 0, hr, queries, sets, slots, num, den, span_len, width)
    oa, w1, den = lax.optimization_barrier((oa, w1, den))
    sent_a = [oa[0], along_y(oa[1], -1), along_y(oa[2], 1), along_y(oa[3], 2)]
    b1 = across(w1, 1)
    ob = attn_far(far_table, bases, hr, hr, queries, sets, slots, num, den, span_len, width)
    ob, w3, sent_a = lax.optimization_barrier((ob, w3, sent_a))
    sent_b = [ob[0], along_y(ob[1], -1), along_y(ob[2], 1), along_y(ob[3], 2)]
    b3 = across(w3, 1)
    xa = combine(sent_a, dec)
    xa, w2 = lax.optimization_barrier((xa, w2))
    xa = lax.all_gather(xa, "tp")
    b2 = across(w2, 1)
    xb = combine(sent_b)
    xb = [xb, along_x(xb, 1), along_x(xb, -1), along_x(xb, 2)]
    mine, theirs = (w1, w3, w2), (b1, b3, b2)
    at = jnp.stack(
        [column * 2 + core, column * 2 + 1 - core, core, column]
        + [(column + d) % tp for d in (3, 1, 2)]
    ).astype(jnp.int32)
    total = reqs * span_len
    out, small = project(at, [xa], out_weight, mine, theirs, total)
    out = project(at, xb, out_weight, mine, theirs, total, out)
    width = out.shape[1]
    return out.reshape(1, reqs, span_len, width), small[: 2 * steps].reshape(1, 2, steps, width)


def solution(mesh):
    placed = (
        P("sec", None, "ctx", "tp"),
        P("sec", None, "ctx", "tp"),
        P("sec", None, "ctx", "tp"),
        P("sec", "ctx", None, "tp"),
        P("sec", "ctx", None, "tp"),
        P("sec", "ctx"),
        P("sec", "ctx"),
        P("sec", None),
        P("sec", "ctx", None, "tp"),
        P("sec", "ctx", None, "tp"),
        P("sec", "ctx", None, "tp"),
        P("sec", "ctx", None, "tp"),
        P("sec", "ctx", None, "tp"),
        P("sec", "ctx"),
        P("sec", "ctx"),
        P("sec", None),
        P("tp", None),
    )
    return jax.shard_map(
        on_device,
        mesh=mesh,
        in_specs=placed,
        out_specs=(P("sec", None, "ctx", "tp"), P("sec", "ctx", None, "tp")),
        check_vma=False,
    )
```

```python
import functools

import jax
import jax.numpy as jnp
from jax import lax
from jax.experimental import pallas as pl
from jax.experimental.pallas import tpu as pltpu
from jax.sharding import PartitionSpec as P

HD = 128
PAGE = 128
BF = jnp.bfloat16
F32 = jnp.float32
NT = (((1,), (1,)), ((), ()))
VM = pl.BlockSpec(memory_space=pltpu.VMEM)
SM = pl.BlockSpec(memory_space=pltpu.SMEM)
HBM = pl.BlockSpec(memory_space=pltpu.HBM)
LITTLE = pl.CostEstimate(flops=1, bytes_accessed=1, transcendentals=0)


def pair_table(ra, rb, tab, cnt, reqs, spans):
    slots = ra.shape[1]
    for r in range(reqs):
        cnt[0, r] = spans

    def count(i, unused):
        for ref in (ra, rb):
            r = ref[0, i]
            cnt[0, r] = cnt[0, r] + 1
        return 0

    lax.fori_loop(0, slots, count, 0)
    total = jnp.int32(0)
    for r in range(reqs):
        tab[3, r] = total
        cnt[1, r] = 2 * total
        n = (cnt[0, r] + 1) // 2

        def owner(p, unused):
            tab[2, p] = r
            tab[1, 2 * p] = 0
            tab[1, 2 * p + 1] = 0
            tab[0, 2 * p] = 0
            tab[0, 2 * p + 1] = 0
            return 0

        lax.fori_loop(total, total + n, owner, 0)
        if spans:
            tab[1, 2 * total] = 200
            cnt[1, r] = 2 * total + 1
        total = total + n
    tab[3, reqs] = total

    def place(i, unused):
        for k, ref in enumerate((ra, rb)):
            r = ref[0, i]
            p = cnt[1, r]
            tab[0, p] = i + k * slots
            tab[1, p] = ref[1, i]
            cnt[1, r] = p + 1
        return 0

    lax.fori_loop(0, slots, place, 0)


def attn_kernel(ra, rb, *refs, first, r0, R, heads, nb):
    *refs, table, cnt = refs
    rows = heads * 128
    half = nb // 2
    if first:
        rel, q_all, ma, mb, num_out, qs_out, den, qv, qs, ks, vs, acc, dacc, p0, p1, sem = refs
    else:
        (bases, qs_in, ma, mb, mc, md, num_in, den_in, o0, o1, o2, o3,
         qs, ks, vs, acc, dacc, p0, p1, tile, stage, sem) = refs
    cs = []

    def copy(src, dst, i):
        c = pltpu.make_async_copy(src, dst, sem.at[i])
        c.start()
        return c

    if first:
        qc = [copy(q_all.at[rel[d]], qv.at[d], 4 + d) for d in range(4)]
        sets = (ma, mb)
    else:
        cs = [copy(qs_in.at[pl.ds(r0, R)], qs, 4), copy(num_in.at[pl.ds(r0, R)], acc, 5)]
        sets = (mc, md)
    for i, m in enumerate(sets):
        cs.append(copy(m.at[pl.ds(0, half)], ks.at[pl.ds(i * half, half)], 2 * i))
        cs.append(copy(m.at[pl.ds(half, half)], vs.at[pl.ds(i * half, half)], 2 * i + 1))
    if not first:
        for i, m in enumerate((ma, mb, mc, md)):
            for j, dst in enumerate((ks, vs)):
                for r in range(R):
                    at = nb + j * 2 + (r0 + r) // 4
                    c = pltpu.make_async_copy(
                        m.at[at, pl.ds((r0 + r) % 4 * 32, 32)],
                        dst.at[nb + r, pl.ds(i * 32, 32)],
                        sem.at[6 + (i * 2 + j) * R + r],
                    )
                    c.start()
                    cs.append(c)
    pair_table(ra, rb, table, cnt, R, 0 if first else 1)
    dacc[...] = jnp.zeros_like(dacc)
    p1[...] = jnp.zeros_like(p1)
    if first:
        acc[...] = jnp.zeros_like(acc)
        for c in qc:
            c.wait()
        for d in range(4):
            for r in range(R):
                for h in range(heads):
                    qs[r, pl.ds(h * 128 + d * 32, 32), :] = qv[d, r, :, pl.ds(h * 128, 128)]
        qs_copy = copy(qs, qs_out, 4)
    else:
        rowi = lax.broadcasted_iota(jnp.int32, (128, 128), 0)
        coli = lax.broadcasted_iota(jnp.int32, (128, 128), 1)

        def pick(i, b):
            g = i // 32
            base = jnp.where(
                g == 0, bases[b], jnp.where(g == 1, bases[b + 1], jnp.where(g == 2, bases[b + 2], bases[b + 3]))
            )
            return base + lax.rem(i, 32)

        tile[...] = jnp.where(pick(rowi, 0) >= pick(coli, 4), coli + 1, 0)
    for c in cs:
        c.wait()
    lane = lax.broadcasted_iota(jnp.int32, (1, 128), 1)
    begin, end = table[3, r0], table[3, r0 + R]

    def pair(p):
        ok = jnp.logical_and(p >= begin, p < end)
        i = jnp.where(ok, 2 * p, 0)
        r = jnp.where(ok, table[2, jnp.where(ok, p, 0)] - r0, 0)
        slots = table[0, i], table[0, i + 1]
        lims = jnp.where(ok, table[1, i], 0), jnp.where(ok, table[1, i + 1], 0)
        return r, slots, lims

    def scores(p, dst):
        r, slots, lims = pair(p)
        if not first:
            slots = [jnp.where(l == 200, nb + r, s) for s, l in zip(slots, lims)]
        K = jnp.concatenate([ks[slots[0]], ks[slots[1]]], axis=0)
        s = lax.dot_general(qs[r], K, NT, preferred_element_type=F32)
        w = jnp.exp(s * HD ** -0.5)
        t = None
        for j in range(2):
            limit = lims[j]
            if first or j:
                keep = (lane < limit)[None]
            else:
                keep = (lane < jnp.where(limit == 200, tile[...], limit))[None]
            one = w[:, j * 128 : (j + 1) * 128].reshape(heads, 128, 128)
            one = jnp.where(keep, one, 0.0).reshape(rows, 128)
            dst[:, j * 128 : (j + 1) * 128] = one.astype(BF)
            t = one if t is None else t + one
        dacc[r] += t

    def products(p, src):
        r, slots, lims = pair(p)
        if not first:
            slots = [jnp.where(l == 200, nb + r, s) for s, l in zip(slots, lims)]
        V = jnp.concatenate([vs[slots[0]], vs[slots[1]]], axis=0)
        acc[r] += jnp.dot(src[...], V, preferred_element_type=F32)

    def step(i, unused):
        p = begin + 2 * i
        products(p - 1, p1)
        scores(p, p0)
        products(p, p0)
        scores(p + 1, p1)
        return 0

    steps = (end - begin + 1) // 2
    lax.fori_loop(0, steps, step, 0)
    products(begin + 2 * steps - 1, p1)

    lane1 = lax.broadcasted_iota(jnp.int32, (128, 128), 1)
    dl = jnp.zeros((128, 128), F32) if first else den_in[...]
    if first:
        num_copy = copy(acc, num_out, 0)
    for r in range(R):
        for h in range(heads):
            col = jnp.sum(dacc[r, pl.ds(h * 128, 128), :], axis=1, keepdims=True)
            dl = dl + jnp.where(lane1 == (r0 + r) * 16 + h, col, 0.0)
    if first:
        den[...] = dl
        num_copy.wait()
        qs_copy.wait()
        return
    outs = [stage.at[d] for d in range(4)]
    for r in range(R):
        for h in range(heads):
            for d in range(4):
                outs[d][r * 32 : r * 32 + 32, h * 128 : h * 128 + 128] = acc[
                    r, h * 128 + d * 32 : h * 128 + d * 32 + 32, :
                ].astype(BF)
    hi = dl.astype(BF)
    lo = (dl - hi.astype(F32)).astype(BF)
    z = jnp.zeros((16, (heads - 4) * 128), BF)
    for d in range(4):
        for k, a in enumerate((hi, lo)):
            outs[d][R * 32 : R * 32 + 16, k * 256 : k * 256 + 128] = a[d * 32 : d * 32 + 16]
            outs[d][R * 32 : R * 32 + 16, k * 256 + 128 : k * 256 + 256] = a[d * 32 + 16 : d * 32 + 32]
        outs[d][R * 32 : R * 32 + 16, 512:] = z
    for c in [copy(stage.at[d], o, d) for d, o in enumerate((o0, o1, o2, o3))]:
        c.wait()


def attn_near(ra, rb, rel, qs, sets, slots):
    R, T, W = qs.shape[1:]
    heads = W // HD
    rows = heads * 128
    nb = 2 * slots
    body = functools.partial(attn_kernel, first=True, r0=0, R=R, heads=heads, nb=nb)
    return pl.pallas_call(
        body,
        in_specs=[SM] * 3 + [HBM] * 3,
        out_specs=[HBM, HBM, VM],
        scratch_shapes=[
            pltpu.VMEM((4, R, T, W), BF),
            pltpu.VMEM((R, rows, 128), BF),
            pltpu.VMEM((nb, 128, 128), BF),
            pltpu.VMEM((nb, 128, 128), BF),
            pltpu.VMEM((R, rows, 128), F32),
            pltpu.VMEM((R, rows, 128), F32),
            pltpu.VMEM((rows, 256), BF),
            pltpu.VMEM((rows, 256), BF),
            pltpu.SemaphoreType.DMA((11,)),
            pltpu.SMEM((4, 80), jnp.int32),
            pltpu.SMEM((2, 16), jnp.int32),
        ],
        out_shape=[
            jax.ShapeDtypeStruct((R, rows, 128), F32),
            jax.ShapeDtypeStruct((R, rows, 128), BF),
            jax.ShapeDtypeStruct((128, 128), F32),
        ],
        compiler_params=pltpu.CompilerParams(vmem_limit_bytes=60 << 20),
        cost_estimate=LITTLE,
        name="attn_near",
    )(ra, rb, rel, qs, *sets)


def attn_far(ra, rb, bases, r0, R, qs, sets, slots, num, den, T, W):
    heads = W // HD
    rows = heads * 128
    nb = 2 * slots
    body = functools.partial(attn_kernel, first=False, r0=r0, R=R, heads=heads, nb=nb)
    return pl.pallas_call(
        body,
        in_specs=[SM] * 3 + [HBM] * 6 + [VM],
        out_specs=[HBM] * 4,
        scratch_shapes=[
            pltpu.VMEM((R, rows, 128), BF),
            pltpu.VMEM((nb + R, 128, 128), BF),
            pltpu.VMEM((nb + R, 128, 128), BF),
            pltpu.VMEM((R, rows, 128), F32),
            pltpu.VMEM((R, rows, 128), F32),
            pltpu.VMEM((rows, 256), BF),
            pltpu.VMEM((rows, 256), BF),
            pltpu.VMEM((128, 128), jnp.int32),
            pltpu.VMEM((4, R * T + 16, W), BF),
            pltpu.SemaphoreType.DMA((6 + 8 * R,)),
            pltpu.SMEM((4, 80), jnp.int32),
            pltpu.SMEM((2, 16), jnp.int32),
        ],
        out_shape=[jax.ShapeDtypeStruct((R * T + 16, W), BF)] * 4,
        compiler_params=pltpu.CompilerParams(vmem_limit_bytes=60 << 20),
        cost_estimate=LITTLE,
        name="attn_far",
    )(ra, rb, bases, qs, *sets, num, den)


def decode_kernel(req, lim, ctx, notes, k_hbm, v_hbm, hand, dk, dv, out, k, v, p, d, o, acc, dacc, sem):
    k_copy = pltpu.make_async_copy(k_hbm, k, sem.at[0])
    v_copy = pltpu.make_async_copy(v_hbm, v, sem.at[1])
    k_copy.start()
    v_copy.start()
    scale = HD ** -0.5
    blocks = k.shape[0]
    handed = hand.shape[1]
    lane = lax.broadcasted_iota(jnp.int32, (1, 128), 1)

    def queries(r):
        return notes[r // 2, pl.ds(pl.multiple_of(r % 2 * 32, 32), 32), :]

    def first_lane(w):
        return jnp.where(lane == 0, jnp.sum(w, axis=1, keepdims=True), 0.0)

    for r in range(handed):
        s = lax.dot_general(queries(r), hand[0, r], NT, preferred_element_type=F32)
        w = jnp.exp(s * scale)
        dacc[r] = first_lane(w)
        acc[r] = jnp.dot(w.astype(BF), hand[1, r], preferred_element_type=F32)
    dacc[handed:] = jnp.zeros_like(dacc[handed:])
    acc[handed:] = jnp.zeros_like(acc[handed:])
    k_copy.wait()
    for i in range(blocks):
        s = lax.dot_general(queries(req[i]), k[i], NT, preferred_element_type=F32)
        w = jnp.where(lane < lim[i], jnp.exp(s * scale), 0.0)
        d[i] = w
        p[i] = w.astype(BF)
    v_copy.wait()
    for i in range(blocks):
        o[i] = jnp.dot(p[i], v[i], preferred_element_type=F32)
    steps = 4
    for j in range(dk.shape[0]):
        r = ctx[0] * dk.shape[0] + j
        s = lax.dot_general(queries(r), dk[j], NT, preferred_element_type=F32)
        row = lax.rem(lax.broadcasted_iota(jnp.int32, s.shape, 0), steps)
        col = lax.broadcasted_iota(jnp.int32, s.shape, 1)
        w = jnp.where(col <= row, jnp.exp(s * scale), 0.0)
        dacc[r] += first_lane(w)
        acc[r] += jnp.dot(w.astype(BF), dv[j], preferred_element_type=F32)
    for i in range(blocks):
        r = req[i]
        acc[r] += o[i]
        dacc[r] += d[i]
    out[:, :, 0:128] = acc[...].astype(BF)
    den = jnp.sum(dacc[...], axis=2, keepdims=True)
    hi = den.astype(BF)
    lo = (den - hi.astype(F32)).astype(BF)
    out[:, :, 128:256] = jnp.where(lane[None] < 64, hi, lo)


def decode(req, lim, ctx, notes, k, v, hand, dk, dv):
    blocks = k.shape[0]
    total = 2 * notes.shape[0]
    return pl.pallas_call(
        decode_kernel,
        in_specs=[SM] * 3 + [VM] + [HBM] * 2 + [VM] * 3,
        out_specs=VM,
        scratch_shapes=[
            pltpu.VMEM(k.shape, BF),
            pltpu.VMEM(v.shape, BF),
            pltpu.VMEM((blocks, 32, 128), BF),
            pltpu.VMEM((blocks, 32, 128), F32),
            pltpu.VMEM((blocks, 32, 128), F32),
            pltpu.VMEM((total, 32, 128), F32),
            pltpu.VMEM((total, 32, 128), F32),
            pltpu.SemaphoreType.DMA((2,)),
        ],
        out_shape=jax.ShapeDtypeStruct((total, 32, 256), BF),
        compiler_params=pltpu.CompilerParams(vmem_limit_bytes=60 << 20),
        cost_estimate=LITTLE,
        name="decode_terms",
    )(req, lim, ctx, notes, k, v, hand, dk, dv)


def combine_kernel(*refs, decode_rows):
    if decode_rows:
        h0, h1, h2, h3, h4, out, parts, small, dec, sem = refs
    else:
        h0, h1, h2, h3, out, parts, sem = refs
    copies = [pltpu.make_async_copy(h, parts.at[i], sem.at[i]) for i, h in enumerate((h0, h1, h2, h3))]
    if decode_rows:
        copies.append(pltpu.make_async_copy(h4, dec, sem.at[4]))
    for c in copies:
        c.start()
    rows = parts.shape[1] - 16
    heads = parts.shape[2] // HD
    if out.shape[0] > rows and not decode_rows:
        out[rows:] = jnp.zeros((out.shape[0] - rows, out.shape[1]), BF)
    for c in copies:
        c.wait()
    if decode_rows:
        sums = jnp.sum(dec[...].astype(F32), axis=0)
        reqs = sums.shape[0]
        dden = sums[:, :, 128:129] + sums[:, :, 192:193]
        att = sums[:, :, :128] / dden
        small[...] = jnp.zeros_like(small)
        for j in range(reqs):
            for h in range(heads):
                small[j * 4 : j * 4 + 4, h * 128 : h * 128 + 128] = att[j, h * 4 : h * 4 + 4]
        out[rows : rows + small.shape[0]] = small[...].astype(BF)

    def total(*at):
        t = parts[(0,) + at].astype(F32)
        for i in range(1, 4):
            t = t + parts[(i,) + at].astype(F32)
        return t

    tail = total(pl.ds(rows, 16), pl.ds(0, 512))
    tail = tail[:, :256] + tail[:, 256:]
    inv = 1.0 / jnp.concatenate([tail[:, :128], tail[:, 128:]], axis=0)
    for r in range(rows // 32):
        for h in range(heads):
            at = (pl.ds(r * 32, 32), pl.ds(h * 128, 128))
            out[at] = (total(*at) * inv[:, r * 16 + h : r * 16 + h + 1]).astype(BF)


def combine(os, dec=None, pad_rows=0):
    rows, width = os[0].shape
    more = [] if dec is None else [dec]
    out_rows = rows if more else rows - 16 + pad_rows
    return pl.pallas_call(
        functools.partial(combine_kernel, decode_rows=len(more)),
        in_specs=[HBM] * (4 + len(more)),
        out_specs=VM,
        scratch_shapes=[pltpu.VMEM((4, rows, width), BF)]
        + ([pltpu.VMEM((16, width), F32), pltpu.VMEM(dec.shape, BF)] if more else [])
        + [pltpu.SemaphoreType.DMA((5,))],
        out_shape=jax.ShapeDtypeStruct((out_rows, width), BF),
        compiler_params=pltpu.CompilerParams(vmem_limit_bytes=60 << 20),
        cost_estimate=pl.CostEstimate(flops=10**6, bytes_accessed=2_500_000, transcendentals=0),
        name="combine",
    )(*os, *more)


def first_kernel(at, x0, x2, w, a2, b2, y, ws, sem):
    depth, half = w.shape[0], ws.shape[2]
    copies = []
    for t, got in enumerate((a2, b2)):
        col = pl.multiple_of(at[t] * half, half)
        for d, part in enumerate((w.at[:, pl.ds(col, half)], got)):
            copies.append(pltpu.make_async_copy(part, ws.at[t, pl.ds(d * depth, depth)], sem.at[t * 2 + d]))
            copies[-1].start()
    x = jnp.concatenate([x0[...], x2[...]], axis=1)
    for t in range(2):
        copies[t * 2].wait()
        copies[t * 2 + 1].wait()
        y[t] = jnp.dot(x, ws[t], preferred_element_type=F32)


def project_first(at, x0, x2, w, a2, b2):
    rows, depth = x0.shape
    half = a2.shape[1]
    return pl.pallas_call(
        first_kernel,
        in_specs=[SM, VM, VM] + [HBM] * 3,
        out_specs=VM,
        out_shape=jax.ShapeDtypeStruct((2, rows, half), F32),
        scratch_shapes=[pltpu.VMEM((2, 2 * depth, half), BF), pltpu.SemaphoreType.DMA((4,))],
        compiler_params=pltpu.CompilerParams(vmem_limit_bytes=60 << 20),
        cost_estimate=LITTLE,
        name="project_first",
    )(at, x0, x2, w, a2, b2)


def project_kernel(at, y0, x1, x3, a1, a3, b1, b3, out, small, ws, y, stage, sem):
    half = stage.shape[2]
    depth = x1.shape[1]
    rows = stage.shape[1]
    copies = []
    for t, parts in enumerate(((a1, a3), (b1, b3))):
        for d, part in enumerate(parts):
            c = pltpu.make_async_copy(part, ws.at[t, pl.ds(d * depth, depth)], sem.at[t * 2 + d])
            c.start()
            copies.append(c)
    y_copy = pltpu.make_async_copy(y0, y, sem.at[6])
    y_copy.start()
    x = jnp.concatenate([x1[...], x3[...]], axis=1)
    outs = []
    for t in range(2):
        side = at[2] if t == 0 else 1 - at[2]
        cols = pl.ds(pl.multiple_of(side * half, half), half)
        copies[t * 2].wait()
        copies[t * 2 + 1].wait()
        total = jnp.dot(x, ws[t], preferred_element_type=F32)
        if t == 0:
            y_copy.wait()
        total = total + y[t]
        stage[t] = total[:rows].astype(BF)
        small[:, cols] = total[rows:].astype(BF)
        c = pltpu.make_async_copy(stage.at[t], out.at[:, cols], sem.at[4 + t])
        c.start()
        outs.append(c)
    for c in outs:
        c.wait()


def project(at, y0, xs, mine, theirs):
    rows, depth = xs[0].shape
    half = mine[0].shape[1]
    rows = rows - 16
    return pl.pallas_call(
        project_kernel,
        in_specs=[SM, HBM] + [VM] * 2 + [HBM] * 4,
        out_specs=[HBM, VM],
        out_shape=[jax.ShapeDtypeStruct((rows, 2 * half), BF), jax.ShapeDtypeStruct((16, 2 * half), BF)],
        scratch_shapes=[
            pltpu.VMEM((2, 2 * depth, half), BF),
            pltpu.VMEM((2, rows + 16, half), F32),
            pltpu.VMEM((2, rows, half), BF),
            pltpu.SemaphoreType.DMA((7,)),
        ],
        compiler_params=pltpu.CompilerParams(vmem_limit_bytes=60 << 20),
        cost_estimate=LITTLE,
        name="project",
    )(at, y0, *xs, *mine, *theirs)


def visible_tokens(req, blk, bounds):
    count = bounds.shape[0]
    hit = req[:, None] == jnp.arange(count, dtype=jnp.int32)[None, :]
    bound = jnp.sum(jnp.where(hit, bounds[None, :], 0), axis=1)
    return jnp.clip(bound - blk * PAGE, 0, PAGE)


def on_device(
    p_query, p_key, p_value, p_cache_k, p_cache_v, p_slot_req, p_slot_blk, p_offsets,
    d_query, d_key, d_value, d_cache_k, d_cache_v, d_slot_req, d_slot_blk, d_lengths, out_weight,
):
    me = lax.axis_index("ctx")
    column = lax.axis_index("tp")
    core = me % 2
    ctx = lax.axis_size("ctx")
    tp = lax.axis_size("tp")

    def along_y(x, d):
        return lax.ppermute(x, "ctx", [(i, i ^ 4 * d) for i in range(ctx)])

    def across(x, bit):
        return lax.ppermute(x, "ctx", [(i, i ^ bit) for i in range(ctx)])

    def along_x(x, d):
        return lax.ppermute(x, "tp", [(i, (i + d) % tp) for i in range(tp)])

    heads = p_query.shape[3] // HD
    reqs, span_len = p_query.shape[1:3]
    slots = p_slot_req.shape[1]
    steps = d_query.shape[2]
    width = heads * HD

    dq = d_query[0].reshape(2, steps, heads, HD).transpose(0, 2, 1, 3).reshape(2, steps * heads, HD)
    dq = jnp.pad(dq, ((0, 0), (0, 32 - steps * heads), (0, 0))).reshape(64, HD)
    dq = jnp.broadcast_to(dq[None], (ctx,) + dq.shape)
    dq, p_key, p_value = lax.optimization_barrier((dq, p_key, p_value))
    notes = lax.all_to_all(dq, "ctx", 0, 0)
    span = jnp.concatenate([p_key[0].reshape(-1, HD), p_value[0].reshape(-1, HD)], axis=0)
    handed = lax.ppermute(span, "sec", [(0, 1), (1, 0)])

    lim0 = visible_tokens(p_slot_req[0], p_slot_blk[0], p_offsets[0])
    note = jnp.pad(jnp.stack([p_slot_req[0], lim0]), ((0, 14), (0, HD - slots))).astype(BF)
    m0 = jnp.concatenate(
        [
            p_cache_k[0].reshape(-1, HD),
            p_cache_v[0].reshape(-1, HD),
            p_key[0].reshape(-1, HD),
            p_value[0].reshape(-1, HD),
            jnp.pad(note, ((0, PAGE - 16), (0, 0))),
        ],
        axis=0,
    ).reshape(-1, PAGE, HD)
    half = out_weight.shape[1] // (2 * tp)
    block = lambda d: lax.dynamic_slice(
        out_weight, (0, (((column + d) % tp) * 2 + core) * half), (out_weight.shape[0], half)
    )
    queries = jnp.broadcast_to(p_query, (ctx // 4,) + p_query.shape[1:])
    m0, queries, notes, handed, a1, a3, a2 = lax.optimization_barrier(
        (m0, queries, notes, handed, block(1), block(3), block(2))
    )
    rings = [[z + 4 * y for y in range(ctx // 4)] for z in range(4)]
    qs = lax.all_to_all(queries, "ctx", 0, 0, axis_index_groups=rings)
    m2 = across(m0, 2)
    m1 = across(m0, 1)
    a1, a3 = along_x(a1, 1), along_x(a3, -1)

    def rows_of(m):
        return m[-1, :2, :slots].astype(jnp.int32)

    rel = jnp.arange(4, dtype=jnp.int32)
    bases = jnp.concatenate([me ^ 4 * rel, me ^ rel]).astype(jnp.int32) * span_len

    pad = ((0, 0), (0, 16 - steps), (0, 0))
    dec = decode(
        d_slot_req[0],
        visible_tokens(d_slot_req[0], d_slot_blk[0], d_lengths[0]),
        me.reshape(1),
        notes,
        d_cache_k[0],
        d_cache_v[0],
        handed.reshape(2, reqs, span_len, HD),
        jnp.pad(d_key[0], pad),
        jnp.pad(d_value[0], pad),
    )
    dec, qs = lax.optimization_barrier((dec, qs))
    dec = lax.all_to_all(dec.reshape(ctx, 2, 32, 256), "ctx", 0, 0)
    num, queries, den = attn_near(rows_of(m0), rows_of(m1), (me // 4) ^ rel, qs, (m0, m1), slots)
    m2, num, queries, den, a1, a3, a2 = lax.optimization_barrier((m2, num, queries, den, a1, a3, a2))
    m3 = across(m2, 1)
    a2 = along_x(a2, 2)
    sets = (m0, m1, m2, m3)
    os = attn_far(rows_of(m2), rows_of(m3), bases, 0, reqs, queries, sets, slots, num, den, span_len, width)
    os, a1, dec = lax.optimization_barrier((os, a1, dec))
    b1 = across(a1, 1)
    x = combine([os[0]] + [along_y(os[d], d) for d in (1, 2, 3)], dec)
    x, b1, a3, a2 = lax.optimization_barrier((x, b1, a3, a2))
    xs = [x, along_x(x, 1), along_x(x, -1), along_x(x, 2)]
    b3, b2 = across(a3, 1), across(a2, 1)
    at = jnp.stack([column * 2 + core, column * 2 + 1 - core, core]).astype(jnp.int32)
    y0 = project_first(at, x, xs[3], out_weight, a2, b2)
    out, small = project(at, y0, xs[1:3], (a1, a3), (b1, b3))
    out_cols = 2 * half
    return out.reshape(1, reqs, span_len, out_cols), small[: 2 * steps].reshape(1, 2, steps, out_cols)


def solution(mesh):
    placed = (
        P("sec", None, "ctx", "tp"),
        P("sec", None, "ctx", "tp"),
        P("sec", None, "ctx", "tp"),
        P("sec", "ctx", None, "tp"),
        P("sec", "ctx", None, "tp"),
        P("sec", "ctx"),
        P("sec", "ctx"),
        P("sec", None),
        P("sec", "ctx", None, "tp"),
        P("sec", "ctx", None, "tp"),
        P("sec", "ctx", None, "tp"),
        P("sec", "ctx", None, "tp"),
        P("sec", "ctx", None, "tp"),
        P("sec", "ctx"),
        P("sec", "ctx"),
        P("sec", None),
        P("tp", None),
    )
    return jax.shard_map(
        on_device,
        mesh=mesh,
        in_specs=placed,
        out_specs=(P("sec", None, "ctx", "tp"), P("sec", "ctx", None, "tp")),
        check_vma=False,
    )
```

```python
import functools

import jax
import jax.numpy as jnp
from jax import lax
from jax.experimental import pallas as pl
from jax.experimental.pallas import tpu as pltpu
from jax.sharding import PartitionSpec as P

HD = 128
PAGE = 128
BF = jnp.bfloat16
F32 = jnp.float32
NT = (((1,), (1,)), ((), ()))
VM = pl.BlockSpec(memory_space=pltpu.VMEM)
SM = pl.BlockSpec(memory_space=pltpu.SMEM)
HBM = pl.BlockSpec(memory_space=pltpu.HBM)
LITTLE = pl.CostEstimate(flops=1, bytes_accessed=1, transcendentals=0)


def pair_table(ra, rb, tab, cnt, reqs, spans):
    slots = ra.shape[1]
    for r in range(reqs):
        cnt[0, r] = spans

    def count(i, unused):
        for ref in (ra, rb):
            r = ref[0, i]
            cnt[0, r] = cnt[0, r] + 1
        return 0

    lax.fori_loop(0, slots, count, 0)
    total = jnp.int32(0)
    for r in range(reqs):
        tab[3, r] = total
        cnt[1, r] = 2 * total
        n = (cnt[0, r] + 1) // 2

        def owner(p, unused):
            tab[2, p] = r
            tab[1, 2 * p] = 0
            tab[1, 2 * p + 1] = 0
            tab[0, 2 * p] = 0
            tab[0, 2 * p + 1] = 0
            return 0

        lax.fori_loop(total, total + n, owner, 0)
        if spans:
            tab[1, 2 * total] = 200
            cnt[1, r] = 2 * total + 1
        total = total + n
    tab[3, reqs] = total

    def place(i, unused):
        for k, ref in enumerate((ra, rb)):
            r = ref[0, i]
            p = cnt[1, r]
            tab[0, p] = i + k * slots
            tab[1, p] = ref[1, i]
            cnt[1, r] = p + 1
        return 0

    lax.fori_loop(0, slots, place, 0)


def attn_kernel(ra, rb, *refs, first, r0, R, heads, nb):
    *refs, table, cnt = refs
    rows = heads * 128
    half = nb // 2
    if first:
        rel, q_all, ma, mb, num_out, qs_out, den, qv, qs, ks, vs, acc, dacc, p0, p1, sem = refs
    else:
        (bases, qs_in, ma, mb, mc, md, num_in, den_in, o0, o1, o2, o3,
         qs, ks, vs, acc, dacc, num, p0, p1, tile, stage, sem) = refs
    cs = []

    def copy(src, dst, i):
        c = pltpu.make_async_copy(src, dst, sem.at[i])
        c.start()
        return c

    if first:
        qc = [copy(q_all.at[rel[d]], qv.at[d], 4 + d) for d in range(4)]
        sets = (ma, mb)
    else:
        cs = [copy(qs_in.at[pl.ds(r0, R)], qs, 4)]
        sets = (mc, md)
    for i, m in enumerate(sets):
        cs.append(copy(m.at[pl.ds(0, half)], ks.at[pl.ds(i * half, half)], 2 * i))
        cs.append(copy(m.at[pl.ds(half, half)], vs.at[pl.ds(i * half, half)], 2 * i + 1))
    if not first:
        for i, m in enumerate((ma, mb, mc, md)):
            for j, dst in enumerate((ks, vs)):
                for r in range(R):
                    at = nb + j * 2 + (r0 + r) // 4
                    c = pltpu.make_async_copy(
                        m.at[at, pl.ds((r0 + r) % 4 * 32, 32)],
                        dst.at[nb + r, pl.ds(i * 32, 32)],
                        sem.at[6 + (i * 2 + j) * R + r],
                    )
                    c.start()
                    cs.append(c)
    pair_table(ra, rb, table, cnt, R, 0 if first else 1)
    dacc[...] = jnp.zeros_like(dacc)
    p1[...] = jnp.zeros_like(p1)
    acc[...] = jnp.zeros_like(acc)
    if first:
        for c in qc:
            c.wait()
        for d in range(4):
            for r in range(R):
                for h in range(heads):
                    qs[r, pl.ds(h * 128 + d * 32, 32), :] = qv[d, r, :, pl.ds(h * 128, 128)]
        qs_copy = copy(qs, qs_out, 4)
    else:
        rowi = lax.broadcasted_iota(jnp.int32, (128, 128), 0)
        coli = lax.broadcasted_iota(jnp.int32, (128, 128), 1)

        def pick(i, b):
            g = i // 32
            base = jnp.where(
                g == 0, bases[b], jnp.where(g == 1, bases[b + 1], jnp.where(g == 2, bases[b + 2], bases[b + 3]))
            )
            return base + lax.rem(i, 32)

        tile[...] = jnp.where(pick(rowi, 0) >= pick(coli, 4), coli + 1, 0)
    for c in cs:
        c.wait()
    if not first:
        num_copy = copy(num_in.at[pl.ds(r0, R)], num, 5)
    lane = lax.broadcasted_iota(jnp.int32, (1, 128), 1)
    begin, end = table[3, r0], table[3, r0 + R]

    def pair(p):
        ok = jnp.logical_and(p >= begin, p < end)
        i = jnp.where(ok, 2 * p, 0)
        r = jnp.where(ok, table[2, jnp.where(ok, p, 0)] - r0, 0)
        slots = table[0, i], table[0, i + 1]
        lims = jnp.where(ok, table[1, i], 0), jnp.where(ok, table[1, i + 1], 0)
        return r, slots, lims

    def scores(p, dst):
        r, slots, lims = pair(p)
        if not first:
            slots = [jnp.where(l == 200, nb + r, s) for s, l in zip(slots, lims)]
        K = jnp.concatenate([ks[slots[0]], ks[slots[1]]], axis=0)
        s = lax.dot_general(qs[r], K, NT, preferred_element_type=F32)
        w = jnp.exp(s * HD ** -0.5)
        t = None
        for j in range(2):
            limit = lims[j]
            if first or j:
                keep = (lane < limit)[None]
            else:
                keep = (lane < jnp.where(limit == 200, tile[...], limit))[None]
            one = w[:, j * 128 : (j + 1) * 128].reshape(heads, 128, 128)
            one = jnp.where(keep, one, 0.0).reshape(rows, 128)
            dst[:, j * 128 : (j + 1) * 128] = one.astype(BF)
            t = one if t is None else t + one
        dacc[r] += t

    def products(p, src):
        r, slots, lims = pair(p)
        if not first:
            slots = [jnp.where(l == 200, nb + r, s) for s, l in zip(slots, lims)]
        V = jnp.concatenate([vs[slots[0]], vs[slots[1]]], axis=0)
        acc[r] += jnp.dot(src[...], V, preferred_element_type=F32)

    def step(i, unused):
        p = begin + 2 * i
        products(p - 1, p1)
        scores(p, p0)
        products(p, p0)
        scores(p + 1, p1)
        return 0

    steps = (end - begin + 1) // 2
    lax.fori_loop(0, steps, step, 0)
    products(begin + 2 * steps - 1, p1)

    lane1 = lax.broadcasted_iota(jnp.int32, (128, 128), 1)
    dl = jnp.zeros((128, 128), F32) if first else den_in[...]
    if first:
        num_copy = copy(acc, num_out, 0)
    for r in range(R):
        for h in range(heads):
            col = jnp.sum(dacc[r, pl.ds(h * 128, 128), :], axis=1, keepdims=True)
            dl = dl + jnp.where(lane1 == (r0 + r) * 16 + h, col, 0.0)
    if first:
        den[...] = dl
        num_copy.wait()
        qs_copy.wait()
        return
    outs = [stage.at[d] for d in range(4)]
    num_copy.wait()
    for r in range(R):
        for h in range(heads):
            for d in range(4):
                sl = pl.ds(h * 128 + d * 32, 32)
                outs[d][r * 32 : r * 32 + 32, h * 128 : h * 128 + 128] = (acc[r, sl, :] + num[r, sl, :]).astype(BF)
    hi = dl.astype(BF)
    lo = (dl - hi.astype(F32)).astype(BF)
    z = jnp.zeros((16, (heads - 4) * 128), BF)
    for d in range(4):
        for k, a in enumerate((hi, lo)):
            outs[d][R * 32 : R * 32 + 16, k * 256 : k * 256 + 128] = a[d * 32 : d * 32 + 16]
            outs[d][R * 32 : R * 32 + 16, k * 256 + 128 : k * 256 + 256] = a[d * 32 + 16 : d * 32 + 32]
        outs[d][R * 32 : R * 32 + 16, 512:] = z
    for c in [copy(stage.at[d], o, d) for d, o in enumerate((o0, o1, o2, o3))]:
        c.wait()


def attn_near(ra, rb, rel, qs, sets, slots):
    R, T, W = qs.shape[1:]
    heads = W // HD
    rows = heads * 128
    nb = 2 * slots
    body = functools.partial(attn_kernel, first=True, r0=0, R=R, heads=heads, nb=nb)
    return pl.pallas_call(
        body,
        in_specs=[SM] * 3 + [HBM] * 3,
        out_specs=[HBM, HBM, VM],
        scratch_shapes=[
            pltpu.VMEM((4, R, T, W), BF),
            pltpu.VMEM((R, rows, 128), BF),
            pltpu.VMEM((nb, 128, 128), BF),
            pltpu.VMEM((nb, 128, 128), BF),
            pltpu.VMEM((R, rows, 128), F32),
            pltpu.VMEM((R, rows, 128), F32),
            pltpu.VMEM((rows, 256), BF),
            pltpu.VMEM((rows, 256), BF),
            pltpu.SemaphoreType.DMA((11,)),
            pltpu.SMEM((4, 80), jnp.int32),
            pltpu.SMEM((2, 16), jnp.int32),
        ],
        out_shape=[
            jax.ShapeDtypeStruct((R, rows, 128), F32),
            jax.ShapeDtypeStruct((R, rows, 128), BF),
            jax.ShapeDtypeStruct((128, 128), F32),
        ],
        compiler_params=pltpu.CompilerParams(vmem_limit_bytes=60 << 20),
        cost_estimate=LITTLE,
        name="attn_near",
    )(ra, rb, rel, qs, *sets)


def attn_far(ra, rb, bases, r0, R, qs, sets, slots, num, den, T, W):
    heads = W // HD
    rows = heads * 128
    nb = 2 * slots
    body = functools.partial(attn_kernel, first=False, r0=r0, R=R, heads=heads, nb=nb)
    return pl.pallas_call(
        body,
        in_specs=[SM] * 3 + [HBM] * 6 + [VM],
        out_specs=[HBM] * 4,
        scratch_shapes=[
            pltpu.VMEM((R, rows, 128), BF),
            pltpu.VMEM((nb + R, 128, 128), BF),
            pltpu.VMEM((nb + R, 128, 128), BF),
            pltpu.VMEM((R, rows, 128), F32),
            pltpu.VMEM((R, rows, 128), F32),
            pltpu.VMEM((R, rows, 128), F32),
            pltpu.VMEM((rows, 256), BF),
            pltpu.VMEM((rows, 256), BF),
            pltpu.VMEM((128, 128), jnp.int32),
            pltpu.VMEM((4, R * T + 16, W), BF),
            pltpu.SemaphoreType.DMA((6 + 8 * R,)),
            pltpu.SMEM((4, 80), jnp.int32),
            pltpu.SMEM((2, 16), jnp.int32),
        ],
        out_shape=[jax.ShapeDtypeStruct((R * T + 16, W), BF)] * 4,
        compiler_params=pltpu.CompilerParams(vmem_limit_bytes=60 << 20),
        cost_estimate=LITTLE,
        name="attn_far",
    )(ra, rb, bases, qs, *sets, num, den)


def decode_kernel(req, lim, ctx, notes, k_hbm, v_hbm, hand, dk, dv, out, k, v, p, d, o, acc, dacc, sem):
    k_copy = pltpu.make_async_copy(k_hbm, k, sem.at[0])
    v_copy = pltpu.make_async_copy(v_hbm, v, sem.at[1])
    k_copy.start()
    v_copy.start()
    scale = HD ** -0.5
    blocks = k.shape[0]
    handed = hand.shape[1]
    lane = lax.broadcasted_iota(jnp.int32, (1, 128), 1)

    def queries(r):
        return notes[r // 2, pl.ds(pl.multiple_of(r % 2 * 32, 32), 32), :]

    def first_lane(w):
        return jnp.where(lane == 0, jnp.sum(w, axis=1, keepdims=True), 0.0)

    for r in range(handed):
        s = lax.dot_general(queries(r), hand[0, r], NT, preferred_element_type=F32)
        w = jnp.exp(s * scale)
        dacc[r] = first_lane(w)
        acc[r] = jnp.dot(w.astype(BF), hand[1, r], preferred_element_type=F32)
    dacc[handed:] = jnp.zeros_like(dacc[handed:])
    acc[handed:] = jnp.zeros_like(acc[handed:])
    k_copy.wait()
    for i in range(blocks):
        s = lax.dot_general(queries(req[i]), k[i], NT, preferred_element_type=F32)
        w = jnp.where(lane < lim[i], jnp.exp(s * scale), 0.0)
        d[i] = w
        p[i] = w.astype(BF)
    v_copy.wait()
    for i in range(blocks):
        o[i] = jnp.dot(p[i], v[i], preferred_element_type=F32)
    steps = 4
    for j in range(dk.shape[0]):
        r = ctx[0] * dk.shape[0] + j
        s = lax.dot_general(queries(r), dk[j], NT, preferred_element_type=F32)
        row = lax.rem(lax.broadcasted_iota(jnp.int32, s.shape, 0), steps)
        col = lax.broadcasted_iota(jnp.int32, s.shape, 1)
        w = jnp.where(col <= row, jnp.exp(s * scale), 0.0)
        dacc[r] += first_lane(w)
        acc[r] += jnp.dot(w.astype(BF), dv[j], preferred_element_type=F32)
    for i in range(blocks):
        r = req[i]
        acc[r] += o[i]
        dacc[r] += d[i]
    out[:, :, 0:128] = acc[...].astype(BF)
    den = jnp.sum(dacc[...], axis=2, keepdims=True)
    hi = den.astype(BF)
    lo = (den - hi.astype(F32)).astype(BF)
    out[:, :, 128:256] = jnp.where(lane[None] < 64, hi, lo)


def decode(req, lim, ctx, notes, k, v, hand, dk, dv):
    blocks = k.shape[0]
    total = 2 * notes.shape[0]
    return pl.pallas_call(
        decode_kernel,
        in_specs=[SM] * 3 + [VM] + [HBM] * 2 + [VM] * 3,
        out_specs=VM,
        scratch_shapes=[
            pltpu.VMEM(k.shape, BF),
            pltpu.VMEM(v.shape, BF),
            pltpu.VMEM((blocks, 32, 128), BF),
            pltpu.VMEM((blocks, 32, 128), F32),
            pltpu.VMEM((blocks, 32, 128), F32),
            pltpu.VMEM((total, 32, 128), F32),
            pltpu.VMEM((total, 32, 128), F32),
            pltpu.SemaphoreType.DMA((2,)),
        ],
        out_shape=jax.ShapeDtypeStruct((total, 32, 256), BF),
        compiler_params=pltpu.CompilerParams(vmem_limit_bytes=60 << 20),
        cost_estimate=LITTLE,
        name="decode_terms",
    )(req, lim, ctx, notes, k, v, hand, dk, dv)


def combine_kernel(*refs, decode_rows):
    if decode_rows:
        h0, h1, h2, h3, h4, out, parts, small, dec, sem = refs
    else:
        h0, h1, h2, h3, out, parts, sem = refs
    copies = [pltpu.make_async_copy(h, parts.at[i], sem.at[i]) for i, h in enumerate((h0, h1, h2, h3))]
    if decode_rows:
        copies.append(pltpu.make_async_copy(h4, dec, sem.at[4]))
    for c in copies:
        c.start()
    rows = parts.shape[1] - 16
    heads = parts.shape[2] // HD
    if out.shape[0] > rows and not decode_rows:
        out[rows:] = jnp.zeros((out.shape[0] - rows, out.shape[1]), BF)
    for c in copies:
        c.wait()
    if decode_rows:
        sums = jnp.sum(dec[...].astype(F32), axis=0)
        reqs = sums.shape[0]
        dden = sums[:, :, 128:129] + sums[:, :, 192:193]
        att = sums[:, :, :128] / dden
        small[...] = jnp.zeros_like(small)
        for j in range(reqs):
            for h in range(heads):
                small[j * 4 : j * 4 + 4, h * 128 : h * 128 + 128] = att[j, h * 4 : h * 4 + 4]
        out[rows : rows + small.shape[0]] = small[...].astype(BF)

    def total(*at):
        t = parts[(0,) + at].astype(F32)
        for i in range(1, 4):
            t = t + parts[(i,) + at].astype(F32)
        return t

    tail = total(pl.ds(rows, 16), pl.ds(0, 512))
    tail = tail[:, :256] + tail[:, 256:]
    inv = 1.0 / jnp.concatenate([tail[:, :128], tail[:, 128:]], axis=0)
    for r in range(rows // 32):
        for h in range(heads):
            at = (pl.ds(r * 32, 32), pl.ds(h * 128, 128))
            out[at] = (total(*at) * inv[:, r * 16 + h : r * 16 + h + 1]).astype(BF)


def combine(os, dec=None, pad_rows=0):
    rows, width = os[0].shape
    more = [] if dec is None else [dec]
    out_rows = rows if more else rows - 16 + pad_rows
    return pl.pallas_call(
        functools.partial(combine_kernel, decode_rows=len(more)),
        in_specs=[HBM] * (4 + len(more)),
        out_specs=VM,
        scratch_shapes=[pltpu.VMEM((4, rows, width), BF)]
        + ([pltpu.VMEM((16, width), F32), pltpu.VMEM(dec.shape, BF)] if more else [])
        + [pltpu.SemaphoreType.DMA((5,))],
        out_shape=jax.ShapeDtypeStruct((out_rows, width), BF),
        compiler_params=pltpu.CompilerParams(vmem_limit_bytes=60 << 20),
        cost_estimate=pl.CostEstimate(flops=10**6, bytes_accessed=2_500_000, transcendentals=0),
        name="combine",
    )(*os, *more)


def first_kernel(at, x0, x2, w, a2, b2, y, ws, sem):
    depth, half = w.shape[0], ws.shape[2]
    copies = []
    for t, got in enumerate((a2, b2)):
        col = pl.multiple_of(at[t] * half, half)
        for d, part in enumerate((w.at[:, pl.ds(col, half)], got)):
            copies.append(pltpu.make_async_copy(part, ws.at[t, pl.ds(d * depth, depth)], sem.at[t * 2 + d]))
            copies[-1].start()
    x = jnp.concatenate([x0[...], x2[...]], axis=1)
    for t in range(2):
        copies[t * 2].wait()
        copies[t * 2 + 1].wait()
        y[t] = jnp.dot(x, ws[t], preferred_element_type=F32)


def project_first(at, x0, x2, w, a2, b2):
    rows, depth = x0.shape
    half = a2.shape[1]
    return pl.pallas_call(
        first_kernel,
        in_specs=[SM, VM, VM] + [HBM] * 3,
        out_specs=VM,
        out_shape=jax.ShapeDtypeStruct((2, rows, half), F32),
        scratch_shapes=[pltpu.VMEM((2, 2 * depth, half), BF), pltpu.SemaphoreType.DMA((4,))],
        compiler_params=pltpu.CompilerParams(vmem_limit_bytes=60 << 20),
        cost_estimate=LITTLE,
        name="project_first",
    )(at, x0, x2, w, a2, b2)


def project_kernel(at, y0, x1, x3, a1, a3, b1, b3, out, small, ws, y, stage, sem):
    half = stage.shape[2]
    depth = x1.shape[1]
    rows = stage.shape[1]
    copies = []
    for t, parts in enumerate(((a1, a3), (b1, b3))):
        for d, part in enumerate(parts):
            c = pltpu.make_async_copy(part, ws.at[t, pl.ds(d * depth, depth)], sem.at[t * 2 + d])
            copies.append(c)
    copies[0].start()
    copies[1].start()
    y_copy = pltpu.make_async_copy(y0, y, sem.at[6])
    y_copy.start()
    x = jnp.concatenate([x1[...], x3[...]], axis=1)
    outs = []
    for t in range(2):
        side = at[2] if t == 0 else 1 - at[2]
        cols = pl.ds(pl.multiple_of(side * half, half), half)
        copies[t * 2].wait()
        copies[t * 2 + 1].wait()
        if t == 0:
            copies[2].start()
            copies[3].start()
        total = jnp.dot(x, ws[t], preferred_element_type=F32)
        if t == 0:
            y_copy.wait()
        total = total + y[t]
        stage[t] = total[:rows].astype(BF)
        small[:, cols] = total[rows:].astype(BF)
        c = pltpu.make_async_copy(stage.at[t], out.at[:, cols], sem.at[4 + t])
        c.start()
        outs.append(c)
    for c in outs:
        c.wait()


def project(at, y0, xs, mine, theirs):
    rows, depth = xs[0].shape
    half = mine[0].shape[1]
    rows = rows - 16
    return pl.pallas_call(
        project_kernel,
        in_specs=[SM, HBM] + [VM] * 2 + [HBM] * 4,
        out_specs=[HBM, VM],
        out_shape=[jax.ShapeDtypeStruct((rows, 2 * half), BF), jax.ShapeDtypeStruct((16, 2 * half), BF)],
        scratch_shapes=[
            pltpu.VMEM((2, 2 * depth, half), BF),
            pltpu.VMEM((2, rows + 16, half), F32),
            pltpu.VMEM((2, rows, half), BF),
            pltpu.SemaphoreType.DMA((7,)),
        ],
        compiler_params=pltpu.CompilerParams(vmem_limit_bytes=60 << 20),
        cost_estimate=LITTLE,
        name="project",
    )(at, y0, *xs, *mine, *theirs)


def visible_tokens(req, blk, bounds):
    count = bounds.shape[0]
    hit = req[:, None] == jnp.arange(count, dtype=jnp.int32)[None, :]
    bound = jnp.sum(jnp.where(hit, bounds[None, :], 0), axis=1)
    return jnp.clip(bound - blk * PAGE, 0, PAGE)


def on_device(
    p_query, p_key, p_value, p_cache_k, p_cache_v, p_slot_req, p_slot_blk, p_offsets,
    d_query, d_key, d_value, d_cache_k, d_cache_v, d_slot_req, d_slot_blk, d_lengths, out_weight,
):
    me = lax.axis_index("ctx")
    column = lax.axis_index("tp")
    core = me % 2
    ctx = lax.axis_size("ctx")
    tp = lax.axis_size("tp")

    def along_y(x, d):
        return lax.ppermute(x, "ctx", [(i, i ^ 4 * d) for i in range(ctx)])

    def across(x, bit):
        return lax.ppermute(x, "ctx", [(i, i ^ bit) for i in range(ctx)])

    def along_x(x, d):
        return lax.ppermute(x, "tp", [(i, (i + d) % tp) for i in range(tp)])

    heads = p_query.shape[3] // HD
    reqs, span_len = p_query.shape[1:3]
    slots = p_slot_req.shape[1]
    steps = d_query.shape[2]
    width = heads * HD

    dq = d_query[0].reshape(2, steps, heads, HD).transpose(0, 2, 1, 3).reshape(2, steps * heads, HD)
    dq = jnp.pad(dq, ((0, 0), (0, 32 - steps * heads), (0, 0))).reshape(64, HD)
    dq = jnp.broadcast_to(dq[None], (ctx,) + dq.shape)
    dq, p_key, p_value = lax.optimization_barrier((dq, p_key, p_value))
    notes = lax.all_to_all(dq, "ctx", 0, 0)
    span = jnp.concatenate([p_key[0].reshape(-1, HD), p_value[0].reshape(-1, HD)], axis=0)
    handed = lax.ppermute(span, "sec", [(0, 1), (1, 0)])

    lim0 = visible_tokens(p_slot_req[0], p_slot_blk[0], p_offsets[0])
    note = jnp.pad(jnp.stack([p_slot_req[0], lim0]), ((0, 14), (0, HD - slots))).astype(BF)
    m0 = jnp.concatenate(
        [
            p_cache_k[0].reshape(-1, HD),
            p_cache_v[0].reshape(-1, HD),
            p_key[0].reshape(-1, HD),
            p_value[0].reshape(-1, HD),
            jnp.pad(note, ((0, PAGE - 16), (0, 0))),
        ],
        axis=0,
    ).reshape(-1, PAGE, HD)
    half = out_weight.shape[1] // (2 * tp)
    block = lambda d: lax.dynamic_slice(
        out_weight, (0, (((column + d) % tp) * 2 + core) * half), (out_weight.shape[0], half)
    )
    queries = jnp.broadcast_to(p_query, (ctx // 4,) + p_query.shape[1:])
    m0, queries, notes, handed, a1, a3, a2 = lax.optimization_barrier(
        (m0, queries, notes, handed, block(1), block(3), block(2))
    )
    rings = [[z + 4 * y for y in range(ctx // 4)] for z in range(4)]
    qs = lax.all_to_all(queries, "ctx", 0, 0, axis_index_groups=rings)
    m2 = across(m0, 2)
    m1 = across(m0, 1)
    a1, a3 = along_x(a1, 1), along_x(a3, -1)

    def rows_of(m):
        return m[-1, :2, :slots].astype(jnp.int32)

    rel = jnp.arange(4, dtype=jnp.int32)
    bases = jnp.concatenate([me ^ 4 * rel, me ^ rel]).astype(jnp.int32) * span_len

    pad = ((0, 0), (0, 16 - steps), (0, 0))
    dec = decode(
        d_slot_req[0],
        visible_tokens(d_slot_req[0], d_slot_blk[0], d_lengths[0]),
        me.reshape(1),
        notes,
        d_cache_k[0],
        d_cache_v[0],
        handed.reshape(2, reqs, span_len, HD),
        jnp.pad(d_key[0], pad),
        jnp.pad(d_value[0], pad),
    )
    dec, qs = lax.optimization_barrier((dec, qs))
    dec = lax.all_to_all(dec.reshape(ctx, 2, 32, 256), "ctx", 0, 0)
    num, queries, den = attn_near(rows_of(m0), rows_of(m1), (me // 4) ^ rel, qs, (m0, m1), slots)
    m2, num, queries, den, a1, a3, a2 = lax.optimization_barrier((m2, num, queries, den, a1, a3, a2))
    m3 = across(m2, 1)
    a2 = along_x(a2, 2)
    sets = (m0, m1, m2, m3)
    os = attn_far(rows_of(m2), rows_of(m3), bases, 0, reqs, queries, sets, slots, num, den, span_len, width)
    os, a1, dec = lax.optimization_barrier((os, a1, dec))
    b1 = across(a1, 1)
    x = combine([os[0]] + [along_y(os[d], d) for d in (1, 2, 3)], dec)
    x, b1, a3, a2 = lax.optimization_barrier((x, b1, a3, a2))
    xs = [x, along_x(x, 1), along_x(x, -1), along_x(x, 2)]
    b3, b2 = across(a3, 1), across(a2, 1)
    at = jnp.stack([column * 2 + core, column * 2 + 1 - core, core]).astype(jnp.int32)
    y0 = project_first(at, x, xs[3], out_weight, a2, b2)
    out, small = project(at, y0, xs[1:3], (a1, a3), (b1, b3))
    out_cols = 2 * half
    return out.reshape(1, reqs, span_len, out_cols), small[: 2 * steps].reshape(1, 2, steps, out_cols)


def solution(mesh):
    placed = (
        P("sec", None, "ctx", "tp"),
        P("sec", None, "ctx", "tp"),
        P("sec", None, "ctx", "tp"),
        P("sec", "ctx", None, "tp"),
        P("sec", "ctx", None, "tp"),
        P("sec", "ctx"),
        P("sec", "ctx"),
        P("sec", None),
        P("sec", "ctx", None, "tp"),
        P("sec", "ctx", None, "tp"),
        P("sec", "ctx", None, "tp"),
        P("sec", "ctx", None, "tp"),
        P("sec", "ctx", None, "tp"),
        P("sec", "ctx"),
        P("sec", "ctx"),
        P("sec", None),
        P("tp", None),
    )
    return jax.shard_map(
        on_device,
        mesh=mesh,
        in_specs=placed,
        out_specs=(P("sec", None, "ctx", "tp"), P("sec", "ctx", None, "tp")),
        check_vma=False,
    )
```
